128 devices in a mesh: row: 16 (over z, y), col: 8 (over x, core).
Axes of the slice: x: 4, y: 4, z: 4, core: 2. Of those that a mesh axis runs over, the one named last changes fastest.
Arguments:
- inputs: bfloat16 [4, 16, 256, 768], P(None, 'row', 'col'), may hold values from -6 to 6
- panel_order: int32 [2], replicated, may hold values from 0 to 63, as said below
Outputs:
- factor_panels: float32 [4, 16, 256, 512], P(None, 'row')
- trailing: float32 [4, 16, 256, 8, 8, 256], P(None, 'row', None, None, 'col')
The draws below stay inside these ranges and needn't reach their ends.
Inputs may be any that keep to these rules, and one draw needn't show every extreme that they name: `panel_order`: 2 distinct tile indices, the last tile 64 - 1 always among them.
All inputs are finite; a program needn't handle non-finite values.
Results may differ from the reference program's by a relative error of at most 0.0003.
Values may be sent and summed in bfloat16 or wider, within the bound.
No kernel may reach another device: no remote copies, remote signals or barrier semaphores. Data moves between devices by JAX's collectives and lax.ppermute only.
A program may use at most 128 MiB of HBM per device.

```python
import math
import jax
import jax.numpy as jnp
from jax import lax

TILE = 256
D0 = 768
TR_DEV = 4
LAYERS = 3
PANELS = 2
NT = 64
TC_DEV = 8
N_ROW = 16
N_COL = 8


def draw_panel_order(key, part):
    key = jax.random.fold_in(key, 7)
    order_key, place_key = jax.random.split(key)
    others = jax.random.permutation(order_key, NT - 1)[:PANELS - 1].astype(jnp.int32)
    place = jax.random.randint(place_key, (), 0, PANELS).astype(jnp.int32)
    slots = jnp.arange(PANELS, dtype=jnp.int32)
    picks = jnp.clip(jnp.where(slots < place, slots, slots - 1), 0, PANELS - 2)
    return jnp.where(slots == place, jnp.int32(NT - 1), others[picks]).astype(jnp.int32)


def levels(rng, extent, shards, least, largest):
    factor_of, own = 1.0, jax.random.fold_in(rng, 6)
    for axis_at, blocks in shards:
        steps = jnp.exp(jax.random.uniform(jax.random.fold_in(own, axis_at), (blocks,), jnp.float32, least / len(shards), largest / len(shards)))
        factor_of = factor_of * jnp.repeat(steps, extent[axis_at] // blocks).reshape([-1 if axis == axis_at else 1 for axis in range(len(extent))])
    return factor_of


def scatter_about(key, shape, deviation, reach, shards=(), kind=jnp.bfloat16):
    gain = levels(key, shape, shards, -0.22, 0.18) if shards else 1.0
    drawn = jax.random.normal(key, shape, jnp.float32) * deviation * gain
    return jnp.minimum(jnp.maximum(drawn, -reach), reach).astype(kind)


def setup_inputs(seed: int = 0) -> dict:
    streams_of = jax.random.split(jax.random.key(seed), 3)
    return {
        "inputs": scatter_about(streams_of[0], (TR_DEV, N_ROW, TILE, D0), 1.0, 6.0, ((1, 16), (2, 8))),
        "panel_order": draw_panel_order(jax.random.fold_in(streams_of[2], 71), 0),
    }


weight_variance = 2.0
bias_variance = 0.1
ridge_term = 0.1

def arc_cosine(kernel, diagonal_rows, diagonal_columns):
    for layer_index in range(LAYERS):
        magnitude = jnp.sqrt(diagonal_rows[:, None] * diagonal_columns[None, :])
        cosine = jnp.clip(kernel / magnitude, -1.0, 1.0)
        theta_angle = jnp.arccos(cosine)
        kernel = bias_variance + weight_variance / (2.0 * math.pi) * magnitude * (jnp.sqrt(1.0 - cosine * cosine) + (math.pi - theta_angle) * cosine)
        diagonal_rows = 0.5 * weight_variance * diagonal_rows + bias_variance
        diagonal_columns = 0.5 * weight_variance * diagonal_columns + bias_variance
    return kernel

def kernel_matrix(inputs):
    flat_inputs = inputs.reshape(-1, D0)
    total_rows = flat_inputs.shape[0]
    squares = lax.optimization_barrier(jnp.sum(jnp.square(flat_inputs.astype(jnp.float32)), axis=1)) / D0
    input_tiles = flat_inputs.reshape(-1, TILE, D0)
    columns = jnp.arange(total_rows, dtype=jnp.int32)

    def one_tile(packed):
        tile_rows, start_row = packed
        kernel = jnp.dot(tile_rows.astype(jnp.float32), flat_inputs.T.astype(jnp.float32), preferred_element_type=jnp.float32) / D0
        diagonal_rows = lax.dynamic_slice_in_dim(squares, start_row, TILE)
        kernel = arc_cosine(kernel, diagonal_rows, squares)
        positions = start_row + jnp.arange(TILE, dtype=jnp.int32)
        return kernel + ridge_term * (positions[:, None] == columns[None, :]).astype(jnp.float32)
    starts = jnp.arange(input_tiles.shape[0], dtype=jnp.int32) * TILE
    return lax.map(one_tile, (input_tiles, starts)).reshape(total_rows, total_rows)

def reference(inputs, panel_order):
    matrix = kernel_matrix(inputs)
    factors = []
    for panel_index in range(PANELS):
        start_row = (panel_order[panel_index] * TILE).astype(jnp.int32)
        panel_slab = lax.dynamic_slice_in_dim(matrix, start_row, TILE, 1)
        pivot_block = lax.dynamic_slice_in_dim(panel_slab, start_row, TILE, 0)
        lower_factor = jnp.linalg.cholesky(pivot_block)
        factor = lax.linalg.triangular_solve(lower_factor, panel_slab, left_side=False, lower=True, transpose_a=True)
        matrix = matrix - jnp.dot(factor, factor.T, precision=lax.Precision.HIGHEST)
        factors.append(factor)
    factor_panels = jnp.concatenate(factors, axis=1).reshape(TR_DEV, N_ROW, TILE, PANELS * TILE)
    trailing = matrix.reshape(TR_DEV, N_ROW, TILE, TC_DEV, N_COL, TILE)
    return (factor_panels, trailing)
```

```python
import math

import jax
import jax.numpy as jnp
from jax import lax
from jax.experimental import pallas as pl
from jax.experimental.pallas import tpu as pltpu
from jax.sharding import PartitionSpec as P

D0 = 768
TILE = 256
PANELS = 2
SPAN = PANELS * TILE
BLOCK = 128
PIVOTS = 8
BIAS = 0.1
RIDGE = 0.1
TINY = 1e-30
EXACT = lax.Precision.HIGHEST
F32 = jnp.float32
BF16 = jnp.bfloat16

ARC = (
    0.30011410855430565,
    0.014911524637152361,
    0.0027575196411184027,
    4.221988638112521e-06,
    0.0005224396428474578,
)


def matmul(left, right, left_dim, right_dim, precision=None):
    return lax.dot_general(
        left, right, (((left_dim,), (right_dim,)), ((), ())), precision=precision,
        preferred_element_type=F32,
    )


def split(value):
    high = value.astype(BF16)
    return high, (value - high.astype(F32)).astype(BF16)


def arc_term(gap):
    series = ARC[4] * gap + ARC[3]
    for coefficient in ARC[2::-1]:
        series = series * gap + coefficient
    return gap * gap * lax.rsqrt(gap) * series


def scales(squares):
    d0 = squares * (1.0 / D0)
    d1 = d0 + BIAS
    d2 = d1 + BIAS
    inverse1 = lax.rsqrt(d1)
    inverse2 = lax.rsqrt(d2)
    root_bias = math.sqrt(BIAS)
    return (
        lax.rsqrt(squares),
        root_bias * inverse1,
        jnp.sqrt(d0) * inverse1,
        root_bias * inverse2,
        jnp.sqrt(d1) * inverse2,
        jnp.sqrt(d2),
    )


def layers(product, rows, columns):
    cosine = product * rows[0] * columns[0]
    gap = jnp.maximum(1.0 - jnp.abs(cosine), TINY)
    value = jnp.maximum(cosine, 0.0) + arc_term(gap)
    for layer in (1, 3):
        gap = 1.0 - rows[layer] * columns[layer]
        gap = jnp.maximum(gap - rows[layer + 1] * columns[layer + 1] * value, TINY)
        value = (1.0 - gap) + arc_term(gap)
    return rows[5] * columns[5] * value


def row_squares(block):
    wide = block.astype(F32)
    return jnp.sum(wide * wide, axis=1, keepdims=True)


def column_squares(block):
    wide = block.astype(F32)
    high, low = split(wide * wide)
    ones = jnp.ones((16, D0), BF16)
    return (matmul(ones, high, 1, 1) + matmul(ones, low, 1, 1))[0:1]


def unit(shape):
    return lax.broadcasted_iota(jnp.int32, shape, 0) == lax.broadcasted_iota(jnp.int32, shape, 1)


def store_scales(squares, out):
    for index, vector in enumerate(scales(squares)):
        out[index] = jnp.broadcast_to(vector, out.shape[1:])


def factor_block(block):
    count = BLOCK // 8
    nb = PIVOTS
    lane = lax.broadcasted_iota(jnp.int32, (8, BLOCK), 1)
    sub = lax.broadcasted_iota(jnp.int32, (8, BLOCK), 0)
    block = list(block)
    inverse = [jnp.where(lane == sub + 8 * g, 1.0, 0.0).astype(F32) for g in range(count)]

    def spread(value):
        return jnp.broadcast_to(value, (8, BLOCK))

    for k in range(0, BLOCK, nb):
        g0, s = k // 8, k % 8
        groups = range(g0 + 1 if s + nb == 8 else g0, count)
        columns = [[None] * count for _ in range(nb)]
        for j in range(nb):
            for g in range(g0, count):
                columns[j][g] = spread(block[g][:, k + j:k + j + 1])
        left = [spread(block[g0][s + j:s + j + 1, :]) for j in range(nb)]
        right = [spread(inverse[g0][s + j:s + j + 1, :]) for j in range(nb)]
        pivot = {
            (i, j): spread(columns[j][g0][s + i:s + i + 1, :])
            for j in range(nb) for i in range(j, nb)
        }
        reciprocal = []
        lower = {}
        for j in range(nb):
            reciprocal.append(1.0 / pivot[j, j])
            for i in range(j + 1, nb):
                lower[i, j] = pivot[i, j] * reciprocal[j]
            for m in range(j + 1, nb):
                for i in range(m, nb):
                    pivot[i, m] = pivot[i, m] - lower[i, j] * pivot[m, j]
        for i in range(nb):
            for j in range(i):
                left[i] = left[i] - lower[i, j] * left[j]
                right[i] = right[i] - lower[i, j] * right[j]
        for g in groups:
            for i in range(nb):
                for j in range(i):
                    columns[i][g] = columns[i][g] - lower[i, j] * columns[j][g]
        left = [left[i] * reciprocal[i] for i in range(nb)]
        scaled = [right[i] * reciprocal[i] for i in range(nb)]
        for g in groups:
            one, two = block[g], inverse[g]
            for i in range(nb):
                if k + nb < BLOCK:
                    one = one - columns[i][g] * left[i]
                two = two - columns[i][g] * scaled[i]
            if g == g0:
                below = sub >= s + nb
                one = jnp.where(below, one, block[g])
                two = jnp.where(below, two, inverse[g])
            block[g], inverse[g] = one, two
        done = inverse[g0]
        for i in range(nb):
            done = jnp.where(sub == s + i, right[i] * lax.rsqrt(pivot[i, i]), done)
        inverse[g0] = done
    return inverse


def invert_factor(matrix, inverse):
    count = SPAN // BLOCK
    inverse[...] = jnp.zeros((SPAN, SPAN), F32)
    for index in range(count):
        o = index * BLOCK
        e = o + BLOCK
        slabs = [matrix[o + 8 * g:o + 8 * g + 8, o:e] for g in range(BLOCK // 8)]
        own = jnp.concatenate(factor_block(slabs), axis=0)
        if index > 0:
            inverse[o:e, 0:o] = matmul(own, inverse[o:e, 0:o], 1, 0, EXACT)
        inverse[o:e, o:e] = own
        if index < count - 1:
            upper = matmul(own, matrix[o:e, e:SPAN], 1, 0, EXACT)
            matrix[e:SPAN, e:SPAN] -= matmul(upper, upper, 0, 0, EXACT)
            inverse[e:SPAN, 0:e] -= matmul(upper, inverse[o:e, 0:e], 0, 0, EXACT)


def pivot_kernel(panel, high_out, low_out, mean_out, mean_row_out, center_out, center_row_out,
                 scales_out, scales_row_out, matrix, inverse):
    store_scales(row_squares(panel[...]), scales_out)
    for index, vector in enumerate(scales(column_squares(panel[...]))):
        scales_row_out[index] = vector
    for index in range(4):
        rows = slice(index * BLOCK, (index + 1) * BLOCK)
        product = matmul(panel[rows, :], panel[...], 1, 1)
        for lanes in range(4):
            columns = slice(lanes * BLOCK, (lanes + 1) * BLOCK)
            matrix[rows, columns] = BIAS + layers(
                product[:, columns],
                [scales_out[i, rows] for i in range(6)],
                [scales_row_out[i, :, columns] for i in range(6)],
            )
    mean_row = jnp.sum(matrix[...], axis=0, keepdims=True) * (1.0 / SPAN)
    mean_row_out[...] = mean_row
    mean = jnp.sum(matrix[...], axis=1, keepdims=True) * (1.0 / SPAN)
    mean_out[...] = jnp.broadcast_to(mean, mean_out.shape)
    matrix[...] += jnp.where(unit((SPAN, SPAN)), RIDGE, 0.0)
    invert_factor(matrix, inverse)
    high, low = split(inverse[...])
    high_out[...] = high
    low_out[...] = low
    center = jnp.sum(inverse[...] * mean_row, axis=1, keepdims=True)
    center_out[...] = jnp.broadcast_to(center, center_out.shape)
    center_row_out[...] = matmul(
        jnp.broadcast_to(mean_row, (8, SPAN)), inverse[...], 1, 1, EXACT
    )[0:1]


def main_kernel(place, row_inputs, column_inputs, panel, high_in, low_in, mean, mean_row, center,
                center_row, panel_scales, panel_scales_row, factor_out, trailing_out,
                column_high, column_low, column_scales, column_shift,
                row_scales, row_high, row_low, product, update):
    q = pl.program_id(0)
    row_position, column_position = place[0], place[1]

    def column_panel(p, _):
        block = column_inputs[p % 2, :, p // 2].reshape(TILE, D0)
        vectors = scales(column_squares(block))
        for index in range(6):
            column_scales[p, index] = vectors[index]
        product[...] = matmul(panel[...], block, 1, 1)

        def chunk(step, _):
            rows = pl.ds(pl.multiple_of(step * 64, 64), 64)
            for half in range(2):
                lanes = slice(half * 128, half * 128 + 128)
                product[rows, lanes] = (BIAS - mean[rows]) + layers(
                    product[rows, lanes],
                    [panel_scales[i, rows] for i in range(6)],
                    [vectors[i][:, lanes] for i in range(6)],
                )
            return 0

        lax.fori_loop(0, SPAN // 64, chunk, 0)
        for index in range(PANELS):
            @pl.when(place[2 + index] == p * 8 + column_position)
            def _():
                rows = slice(index * TILE, (index + 1) * TILE)
                product[rows, :] += jnp.where(unit((TILE, TILE)), RIDGE, 0.0)

        high, low = split(product[...])
        pieces = []
        for index in range(PANELS):
            rows = slice(index * TILE, (index + 1) * TILE)
            depth = (index + 1) * TILE
            pieces.append(
                matmul(high_in[rows, :depth], high[:depth], 1, 0)
                + (matmul(high_in[rows, :depth], low[:depth], 1, 0)
                   + matmul(low_in[rows, :depth], high[:depth], 1, 0))
            )
        factor = jnp.concatenate(pieces, axis=0)
        shift = 0.0
        for start in range(0, SPAN, 128):
            part = factor[start:start + 128]
            weight = center[start:start + 128]
            shift = shift + jnp.sum(
                part * jnp.concatenate([weight, weight], axis=1), axis=0, keepdims=True
            )
        column_shift[p] = shift
        high, low = split(factor)
        column_high[p] = high
        column_low[p] = low
        return 0

    @pl.when(q == 0)
    def _():
        lax.fori_loop(0, 8, column_panel, 0)

    own = row_inputs[:, 0].reshape(TILE, D0)
    store_scales(row_squares(own), row_scales)
    base = jnp.sum(center_row[...] * center_row[...], axis=1, keepdims=True)
    for index in range(PANELS):
        product[:TILE, :] = matmul(own, panel[index * TILE:(index + 1) * TILE, :], 1, 1)

        def chunk(step, _):
            rows = pl.ds(pl.multiple_of(step * 64, 64), 64)
            for half in range(2):
                lanes = slice(half * 128, half * 128 + 128)
                wide = slice(index * TILE + half * 128, index * TILE + half * 128 + 128)
                product[rows, lanes] = (BIAS - mean_row[:, wide]) + layers(
                    product[rows, lanes],
                    [row_scales[i, rows] for i in range(6)],
                    [panel_scales_row[i, :, wide] for i in range(6)],
                )
            return 0

        lax.fori_loop(0, TILE // 64, chunk, 0)

        @pl.when(place[2 + index] == q * 16 + row_position)
        def _():
            product[:TILE, :] += jnp.where(unit((TILE, TILE)), RIDGE, 0.0)

        high, low = split(product[:TILE, :])
        row_high[:, index * TILE:(index + 1) * TILE] = high
        row_low[:, index * TILE:(index + 1) * TILE] = low
    pieces = []
    for index in range(PANELS):
        rows = slice(index * TILE, (index + 1) * TILE)
        depth = (index + 1) * TILE
        high, low = row_high[:, :depth], row_low[:, :depth]
        pieces.append(
            matmul(high, high_in[rows, :depth], 1, 1)
            + (matmul(high, low_in[rows, :depth], 1, 1)
               + matmul(low, high_in[rows, :depth], 1, 1))
        )
    factor = jnp.concatenate(pieces, axis=1)
    factor_out[0] = factor + center_row[...]
    shift = (BIAS - base) - jnp.sum(factor * center_row[...], axis=1, keepdims=True)
    row_scales[6] = jnp.broadcast_to(shift, (TILE, 128))
    high, low = split(factor)
    row_high[...] = high
    row_low[...] = low

    def tile(p, _):
        block = column_inputs[p % 2, :, p // 2].reshape(TILE, D0)
        product[:TILE, :] = matmul(own, block, 1, 1)
        update[...] = matmul(row_high[...], column_high[p], 1, 0) + (
            matmul(row_high[...], column_low[p], 1, 0) + matmul(row_low[...], column_high[p], 1, 0)
        )

        @pl.when(q * 16 + row_position == p * 8 + column_position)
        def _():
            update[...] -= jnp.where(unit((TILE, TILE)), RIDGE, 0.0)

        def chunk(step, _):
            start = pl.multiple_of(step * 64, 64)
            rows = pl.ds(start, 64)
            for half in range(2):
                lanes = slice(half * 128, half * 128 + 128)
                value = layers(
                    product[rows, lanes],
                    [row_scales[i, rows] for i in range(6)],
                    [column_scales[p, i, :, lanes] for i in range(6)],
                )
                value = value + (row_scales[6, rows] - column_shift[p, :, lanes])
                value = value - update[rows, lanes]
                trailing_out[pl.ds(start * 16 + p * 2 + half, 64, stride=16), :] = value
            return 0

        lax.fori_loop(0, TILE // 64, chunk, 0)
        return 0

    lax.fori_loop(0, 8, tile, 0)


def whole(shape):
    return pl.BlockSpec(shape, lambda *_: (0,) * len(shape))


def call_pivot(panel):
    shapes = [
        ((SPAN, SPAN), BF16), ((SPAN, SPAN), BF16), ((SPAN, 128), F32), ((1, SPAN), F32),
        ((SPAN, 128), F32), ((1, SPAN), F32), ((6, SPAN, 128), F32), ((6, 1, SPAN), F32),
    ]
    return pl.pallas_call(
        pivot_kernel,
        out_shape=[jax.ShapeDtypeStruct(s, d) for s, d in shapes],
        scratch_shapes=[pltpu.VMEM((SPAN, SPAN), F32), pltpu.VMEM((SPAN, SPAN), F32)],
        compiler_params=pltpu.CompilerParams(vmem_limit_bytes=40 * 2**20),
        name="pivot",
    )(panel)


def call_main(place, row_inputs, column_inputs, panel, pivot):
    arrays = (panel, *pivot)
    return pl.pallas_call(
        main_kernel,
        grid=(4,),
        out_shape=[
            jax.ShapeDtypeStruct((4, TILE, SPAN), F32),
            jax.ShapeDtypeStruct((4 * TILE * 16, 128), F32),
        ],
        in_specs=[
            pl.BlockSpec(memory_space=pltpu.SMEM),
            pl.BlockSpec((8, 1, 32, D0), lambda q: (0, q, 0, 0)),
            whole((2, 8, 4, 32, D0)),
        ] + [whole(a.shape) for a in arrays],
        out_specs=[
            pl.BlockSpec((1, TILE, SPAN), lambda q: (q, 0, 0)),
            pl.BlockSpec((TILE * 16, 128), lambda q: (q, 0)),
        ],
        scratch_shapes=[
            pltpu.VMEM((8, SPAN, TILE), BF16),
            pltpu.VMEM((8, SPAN, TILE), BF16),
            pltpu.VMEM((8, 6, 1, TILE), F32),
            pltpu.VMEM((8, 1, TILE), F32),
            pltpu.VMEM((7, TILE, 128), F32),
            pltpu.VMEM((TILE, SPAN), BF16),
            pltpu.VMEM((TILE, SPAN), BF16),
            pltpu.VMEM((SPAN, TILE), F32),
            pltpu.VMEM((TILE, TILE), F32),
        ],
        compiler_params=pltpu.CompilerParams(vmem_limit_bytes=56 * 2**20),
        name="main",
    )(place, row_inputs, column_inputs, *arrays)


def exchange(block, axis, count):
    return lax.all_to_all(
        jnp.broadcast_to(block[None], (count,) + block.shape), axis, 0, 0, tiled=True
    )


def per_device(inputs, panel_order):
    own = inputs[:, 0]
    row_count = lax.axis_size("row")
    column_count = lax.axis_size("col")
    row_position = lax.axis_index("row")
    column_position = lax.axis_index("col")
    chosen = jnp.stack([
        lax.dynamic_index_in_dim(own, panel_order[k] // row_count, 0, keepdims=False)
        for k in range(PANELS)
    ])
    sent = chosen.reshape(PANELS, row_count, 2, D0).transpose(1, 0, 2, 3)
    came = lax.all_to_all(sent, "row", 0, 0, tiled=True)
    piece = jnp.stack([
        lax.dynamic_index_in_dim(came[:, k], panel_order[k] % row_count, 0, keepdims=False)
        for k in range(PANELS)
    ])
    gathered = exchange(piece, ("col", "row"), row_count * column_count)
    panel = gathered.transpose(1, 0, 2, 3).reshape(SPAN, D0)
    turn = [
        (r * column_count + c, (column_count * (r // column_count) + c) * column_count + r % column_count)
        for r in range(row_count) for c in range(column_count)
    ]
    row_inputs = exchange(own, "col", column_count)
    turned = lax.ppermute(own, ("row", "col"), turn)
    column_inputs = exchange(turned, "row", row_count).reshape(2, 8, 4, 32, D0)
    place = jnp.concatenate([
        jnp.stack([row_position, column_position]).astype(jnp.int32), panel_order
    ])
    pivot = call_pivot(panel)
    factor, trailing = call_main(place, row_inputs, column_inputs, panel, pivot)
    return factor.reshape(4, 1, TILE, SPAN), trailing.reshape(4, 1, TILE, 8, 1, TILE)


def solution(mesh):
    in_specs = (P(None, "row", "col", None), P())
    out_specs = (P(None, "row", None, None), P(None, "row", None, None, "col", None))
    return jax.shard_map(
        per_device, mesh=mesh, in_specs=in_specs, out_specs=out_specs, check_vma=False
    )
```

```python
import math

import jax
import jax.numpy as jnp
from jax import lax
from jax.experimental import pallas as pl
from jax.experimental.pallas import tpu as pltpu
from jax.sharding import PartitionSpec as P

D0 = 768
TILE = 256
PANELS = 2
SPAN = PANELS * TILE
BLOCK = 128
PIVOTS = 8
BIAS = 0.1
RIDGE = 0.1
TINY = 1e-30
EXACT = lax.Precision.HIGHEST
F32 = jnp.float32
BF16 = jnp.bfloat16

ARC = (
    0.30011410855430565,
    0.014911524637152361,
    0.0027575196411184027,
    4.221988638112521e-06,
    0.0005224396428474578,
)


def matmul(left, right, left_dim, right_dim, precision=None):
    return lax.dot_general(
        left, right, (((left_dim,), (right_dim,)), ((), ())), precision=precision,
        preferred_element_type=F32,
    )


def split(value):
    high = value.astype(BF16)
    return high, (value - high.astype(F32)).astype(BF16)


def arc_term(gap):
    series = ARC[4] * gap + ARC[3]
    for coefficient in ARC[2::-1]:
        series = series * gap + coefficient
    return gap * gap * lax.rsqrt(gap) * series


def scales(squares):
    d0 = squares * (1.0 / D0)
    d1 = d0 + BIAS
    d2 = d1 + BIAS
    inverse1 = lax.rsqrt(d1)
    inverse2 = lax.rsqrt(d2)
    root_bias = math.sqrt(BIAS)
    return (
        lax.rsqrt(squares),
        root_bias * inverse1,
        jnp.sqrt(d0) * inverse1,
        root_bias * inverse2,
        jnp.sqrt(d1) * inverse2,
        jnp.sqrt(d2),
    )


def layers(product, rows, columns):
    cosine = product * rows[0] * columns[0]
    gap = jnp.maximum(1.0 - jnp.abs(cosine), TINY)
    value = jnp.maximum(cosine, 0.0) + arc_term(gap)
    for layer in (1, 3):
        gap = 1.0 - rows[layer] * columns[layer]
        gap = jnp.maximum(gap - rows[layer + 1] * columns[layer + 1] * value, TINY)
        value = (1.0 - gap) + arc_term(gap)
    return rows[5] * columns[5] * value


def row_squares(block):
    wide = block.astype(F32)
    return jnp.sum(wide * wide, axis=1, keepdims=True)


def column_squares(block):
    wide = block.astype(F32)
    high, low = split(wide * wide)
    ones = jnp.ones((16, D0), BF16)
    return (matmul(ones, high, 1, 1) + matmul(ones, low, 1, 1))[0:1]


def unit(shape):
    return lax.broadcasted_iota(jnp.int32, shape, 0) == lax.broadcasted_iota(jnp.int32, shape, 1)


def store_scales(squares, out):
    for index, vector in enumerate(scales(squares)):
        out[index] = jnp.broadcast_to(vector, out.shape[1:])


def factor_block(block):
    count = BLOCK // 8
    nb = PIVOTS
    lane = lax.broadcasted_iota(jnp.int32, (8, BLOCK), 1)
    sub = lax.broadcasted_iota(jnp.int32, (8, BLOCK), 0)
    block = list(block)
    inverse = [jnp.where(lane == sub + 8 * g, 1.0, 0.0).astype(F32) for g in range(count)]

    def spread(value):
        return jnp.broadcast_to(value, (8, BLOCK))

    for k in range(0, BLOCK, nb):
        g0, s = k // 8, k % 8
        groups = range(g0 + 1 if s + nb == 8 else g0, count)
        columns = [[None] * count for _ in range(nb)]
        for j in range(nb):
            for g in range(g0, count):
                columns[j][g] = spread(block[g][:, k + j:k + j + 1])
        left = [spread(block[g0][s + j:s + j + 1, :]) for j in range(nb)]
        right = [spread(inverse[g0][s + j:s + j + 1, :]) for j in range(nb)]
        pivot = {
            (i, j): spread(columns[j][g0][s + i:s + i + 1, :])
            for j in range(nb) for i in range(j, nb)
        }
        reciprocal = []
        lower = {}
        for j in range(nb):
            reciprocal.append(1.0 / pivot[j, j])
            for i in range(j + 1, nb):
                lower[i, j] = pivot[i, j] * reciprocal[j]
            for m in range(j + 1, nb):
                for i in range(m, nb):
                    pivot[i, m] = pivot[i, m] - lower[i, j] * pivot[m, j]
        for i in range(nb):
            for j in range(i):
                left[i] = left[i] - lower[i, j] * left[j]
                right[i] = right[i] - lower[i, j] * right[j]
        for g in groups:
            for i in range(nb):
                for j in range(i):
                    columns[i][g] = columns[i][g] - lower[i, j] * columns[j][g]
        left = [left[i] * reciprocal[i] for i in range(nb)]
        scaled = [right[i] * reciprocal[i] for i in range(nb)]
        for g in groups:
            one, two = block[g], inverse[g]
            for i in range(nb):
                if k + nb < BLOCK:
                    one = one - columns[i][g] * left[i]
                two = two - columns[i][g] * scaled[i]
            if g == g0:
                below = sub >= s + nb
                one = jnp.where(below, one, block[g])
                two = jnp.where(below, two, inverse[g])
            block[g], inverse[g] = one, two
        done = inverse[g0]
        for i in range(nb):
            done = jnp.where(sub == s + i, right[i] * lax.rsqrt(pivot[i, i]), done)
        inverse[g0] = done
    return inverse


def invert_factor(matrix, inverse):
    count = SPAN // BLOCK
    inverse[...] = jnp.zeros((SPAN, SPAN), F32)
    for index in range(count):
        o = index * BLOCK
        e = o + BLOCK
        slabs = [matrix[o + 8 * g:o + 8 * g + 8, o:e] for g in range(BLOCK // 8)]
        own = jnp.concatenate(factor_block(slabs), axis=0)
        if index > 0:
            inverse[o:e, 0:o] = matmul(own, inverse[o:e, 0:o], 1, 0, EXACT)
        inverse[o:e, o:e] = own
        if index < count - 1:
            upper = matmul(own, matrix[o:e, e:SPAN], 1, 0, EXACT)
            matrix[e:SPAN, e:SPAN] -= matmul(upper, upper, 0, 0, EXACT)
            inverse[e:SPAN, 0:e] -= matmul(upper, inverse[o:e, 0:e], 0, 0, EXACT)


def choose_kernel(order, own, out):
    for k in range(PANELS):
        rows = own[order[k] // 16].astype(F32)
        for device in range(16):
            start = device % 4 * 8
            out[device, k] = rows[start:start + 8].astype(BF16)


def pick_kernel(order, came, out):
    for k in range(PANELS):
        rows = came[order[k] % 16, k]
        for device in range(16):
            out[device, k] = rows


def pivot_kernel(mine, other, panel, high_out, low_out, mean_out, mean_row_out, center_out, center_row_out,
                 scales_out, scales_row_out, matrix, inverse):
    core = lax.axis_index("col") % 2
    for source, side in ((mine, core), (other, 1 - core)):
        for k in range(PANELS):
            for x in range(4):
                for y in (0, 2):
                    rows = [source[(y + i) * 4 + x, k].astype(F32) for i in range(2)]
                    start = pl.multiple_of(k * TILE + 64 * x + 32 * side + 8 * y, 16)
                    panel[pl.ds(start, 16), :] = jnp.concatenate(rows, axis=0).astype(BF16)
    store_scales(row_squares(panel[...]), scales_out)
    for index, vector in enumerate(scales(column_squares(panel[...]))):
        scales_row_out[index] = vector
    for index in range(4):
        rows = slice(index * BLOCK, (index + 1) * BLOCK)
        product = matmul(panel[rows, :], panel[...], 1, 1)
        for lanes in range(4):
            columns = slice(lanes * BLOCK, (lanes + 1) * BLOCK)
            matrix[rows, columns] = BIAS + layers(
                product[:, columns],
                [scales_out[i, rows] for i in range(6)],
                [scales_row_out[i, :, columns] for i in range(6)],
            )
    mean_row = jnp.sum(matrix[...], axis=0, keepdims=True) * (1.0 / SPAN)
    mean_row_out[...] = mean_row
    mean = jnp.sum(matrix[...], axis=1, keepdims=True) * (1.0 / SPAN)
    mean_out[...] = jnp.broadcast_to(mean, mean_out.shape)
    matrix[...] += jnp.where(unit((SPAN, SPAN)), RIDGE, 0.0)
    invert_factor(matrix, inverse)
    high, low = split(inverse[...])
    high_out[...] = high
    low_out[...] = low
    center = jnp.sum(inverse[...] * mean_row, axis=1, keepdims=True)
    center_out[...] = jnp.broadcast_to(center, center_out.shape)
    center_row_out[...] = matmul(
        jnp.broadcast_to(mean_row, (8, SPAN)), inverse[...], 1, 1, EXACT
    )[0:1]


def eye_term(start, lanes, amount):
    row = lax.broadcasted_iota(jnp.int32, (64, 128), 0) + (start - lanes)
    return jnp.where(row == lax.broadcasted_iota(jnp.int32, (64, 128), 1), amount, 0.0)


def main_kernel(order, row_inputs, column_inputs, panel,
                high_in, low_in, mean, mean_row, center, center_row, panel_scales,
                panel_scales_row, factor_out, trailing_out,
                column_high, column_low, column_scales, column_shift,
                own, row_scales, row_high, row_low, row_factor,
                product0, product1, update0, update1, high0, high1, low0, low1):
    group = pl.program_id(0)
    row_position, column_position = lax.axis_index("row"), lax.axis_index("col")
    product, update = (product0, product1), (update0, update1)
    panel_high, panel_low = (high0, high1), (low0, low1)

    def column_block(p):
        return column_inputs[p % 2, :, p // 2].reshape(TILE, D0)

    def ridge_of(tile, index):
        return jnp.where(order[index] == tile, RIDGE, 0.0).astype(F32)

    def column_first(p, slot):
        block = column_block(p)
        product[slot][...] = matmul(panel[...], block, 1, 1)
        for index, vector in enumerate(scales(column_squares(block))):
            column_scales[p, index] = vector

    def column_middle(p, slot):
        for start in range(0, SPAN, 64):
            index = start // TILE
            ridge = ridge_of(p * 8 + column_position, index)
            rows = slice(start, start + 64)
            for lanes in (0, 128):
                wide = slice(lanes, lanes + 128)
                value = (BIAS - mean[rows]) + layers(
                    product[slot][rows, wide],
                    [panel_scales[i, rows] for i in range(6)],
                    [column_scales[p, i, :, wide] for i in range(6)],
                )
                if start % TILE // 128 * 128 == lanes:
                    value = value + eye_term(start % TILE, lanes, ridge)
                high, low = split(value)
                panel_high[slot][rows, wide] = high
                panel_low[slot][rows, wide] = low

    def column_last(p, slot):
        shift = 0.0
        for index in range(PANELS):
            rows = slice(index * TILE, (index + 1) * TILE)
            depth = (index + 1) * TILE
            high, low = panel_high[slot][:depth, :], panel_low[slot][:depth, :]
            factor = matmul(high_in[rows, :depth], high, 1, 0) + (
                matmul(high_in[rows, :depth], low, 1, 0) + matmul(low_in[rows, :depth], high, 1, 0)
            )
            weight = center[rows]
            shift = shift + jnp.sum(
                factor * jnp.concatenate([weight, weight], axis=1), axis=0, keepdims=True
            )
            high, low = split(factor)
            column_high[p, rows] = high
            column_low[p, rows] = low
        column_shift[p] = shift

    def row_first(q, slot):
        block = own[pl.ds(pl.multiple_of(q * TILE, TILE), TILE), :]
        for index in range(PANELS):
            rows = slice(index * TILE, (index + 1) * TILE)
            product[slot][rows, :] = matmul(block, panel[rows, :], 1, 1)

    def row_middle(q, slot):
        for index in range(PANELS):
            ridge = ridge_of(q * 16 + row_position, index)
            for start in range(0, TILE, 64):
                rows = pl.ds(pl.multiple_of(q * TILE + start, 64), 64)
                here = slice(index * TILE + start, index * TILE + start + 64)
                for lanes in (0, 128):
                    wide = slice(index * TILE + lanes, index * TILE + lanes + 128)
                    value = (BIAS - mean_row[:, wide]) + layers(
                        product[slot][here, lanes:lanes + 128],
                        [row_scales[i, rows] for i in range(6)],
                        [panel_scales_row[i, :, wide] for i in range(6)],
                    )
                    if start // 128 * 128 == lanes:
                        value = value + eye_term(start, lanes, ridge)
                    high, low = split(value)
                    panel_high[slot][here, lanes:lanes + 128] = high
                    panel_low[slot][here, lanes:lanes + 128] = low

    def row_last(q, slot):
        rows = pl.ds(pl.multiple_of(q * TILE, TILE), TILE)
        shift = BIAS - jnp.sum(center_row[...] * center_row[...], axis=1, keepdims=True)
        for index in range(PANELS):
            wide = slice(index * TILE, (index + 1) * TILE)
            factor = 0.0
            for part in range(index + 1):
                depth = slice(part * TILE, (part + 1) * TILE)
                high, low = panel_high[slot][depth, :], panel_low[slot][depth, :]
                factor = factor + (
                    matmul(high, high_in[wide, depth], 1, 1)
                    + (matmul(high, low_in[wide, depth], 1, 1) + matmul(low, high_in[wide, depth], 1, 1))
                )
            row_factor[rows, wide] = factor + center_row[:, wide]
            shift = shift - jnp.sum(factor * center_row[:, wide], axis=1, keepdims=True)
            high, low = split(factor)
            row_high[rows, wide] = high
            row_low[rows, wide] = low
        row_scales[6, rows] = jnp.broadcast_to(shift, (TILE, 128))

    def pipeline(count, first, middle, last):
        first(0, 0)

        def pair(step, _):
            for slot in range(2):
                at = step * 2 + slot
                last(jnp.maximum(at - 1, 0), 1 - slot)
                first(jnp.minimum(at + 1, count - 1), 1 - slot)
                middle(at, slot)
            return 0

        lax.fori_loop(0, count // 2, pair, 0)
        last(count - 1, 1)

    @pl.when(group == 0)
    def _():
        for q in range(4):
            own[q * TILE:(q + 1) * TILE, :] = row_inputs[:, q].reshape(TILE, D0)
        for start in range(0, 4 * TILE, 128):
            for index, vector in enumerate(scales(row_squares(own[start:start + 128, :]))):
                row_scales[index, start:start + 128] = jnp.broadcast_to(vector, (128, 128))
        pipeline(4, row_first, row_middle, row_last)
        pipeline(8, column_first, column_middle, column_last)

    for half in range(2):
        rows = pl.ds(pl.multiple_of(group * 2 * TILE + half * TILE, TILE), TILE)
        factor_out[half] = row_factor[rows, :]

    def tile_first(p, slot):
        rows = slice(slot * SPAN, (slot + 1) * SPAN)
        product[slot][...] = matmul(own[rows, :], column_block(p), 1, 1)
        update[slot][...] = matmul(row_high[rows, :], column_high[p], 1, 0) + (
            matmul(row_high[rows, :], column_low[p], 1, 0)
            + matmul(row_low[rows, :], column_high[p], 1, 0)
        )

    def tile_middle(p, slot):
        for start in range(0, SPAN, 64):
            here = slice(start, start + 64)
            rows = slice(slot * SPAN + start, slot * SPAN + start + 64)
            for half in range(2):
                wide = slice(half * 128, half * 128 + 128)
                value = layers(
                    product[slot][here, wide],
                    [row_scales[i, rows] for i in range(6)],
                    [column_scales[p, i, :, wide] for i in range(6)],
                )
                value = value + (row_scales[6, rows] - column_shift[p, :, wide])
                value = value - update[slot][here, wide]
                trailing_out[rows, p % 4 * 2 + half, :] = value

    tile_first(group * 4, 0)

    def tile(step, _):
        p = group * 4 + step
        tile_first(p, 1)
        tile_middle(p, 0)
        tile_first(jnp.minimum(p + 1, 7), 0)
        tile_middle(p, 1)
        return 0

    lax.fori_loop(0, 4, tile, 0)

    @pl.when(row_position % 8 == column_position)
    def _():
        for part in range(2):
            q = group * 2 + part
            p = part * 2 + row_position // 8
            for start in range(0, TILE, 64):
                half = start // 128
                at = pl.ds(pl.multiple_of(q * TILE + start, 64), 64)
                trailing_out[at, p * 2 + half, :] += eye_term(start, half * 128, RIDGE)


def whole(shape):
    return pl.BlockSpec(shape, lambda *_: (0,) * len(shape))


def call_small(kernel, order, block, name):
    return pl.pallas_call(
        kernel,
        out_shape=jax.ShapeDtypeStruct((16, PANELS, 8, D0), BF16),
        in_specs=[pl.BlockSpec(memory_space=pltpu.SMEM), pl.BlockSpec(memory_space=pltpu.VMEM)],
        name=name,
    )(order, block)


def call_pivot(mine, other):
    shapes = [
        ((SPAN, D0), BF16),
        ((SPAN, SPAN), BF16), ((SPAN, SPAN), BF16), ((SPAN, 128), F32), ((1, SPAN), F32),
        ((SPAN, 128), F32), ((1, SPAN), F32), ((6, SPAN, 128), F32), ((6, 1, SPAN), F32),
    ]
    return pl.pallas_call(
        pivot_kernel,
        out_shape=[jax.ShapeDtypeStruct(s, d) for s, d in shapes],
        in_specs=[pl.BlockSpec(memory_space=pltpu.VMEM)] * 2,
        scratch_shapes=[pltpu.VMEM((SPAN, SPAN), F32), pltpu.VMEM((SPAN, SPAN), F32)],
        compiler_params=pltpu.CompilerParams(vmem_limit_bytes=60 * 2**20),
        cost_estimate=pl.CostEstimate(flops=3 * 10**10, bytes_accessed=4 * 10**6, transcendentals=0),
        name="pivot",
    )(mine, other)


def call_main(order, row_inputs, column_inputs, arrays):
    factor, trailing = pl.pallas_call(
        main_kernel,
        grid=(2,),
        out_shape=[
            jax.ShapeDtypeStruct((4, TILE, SPAN), F32),
            jax.ShapeDtypeStruct((4 * TILE, 16, 128), F32),
        ],
        in_specs=[pl.BlockSpec(memory_space=pltpu.SMEM)]
        + [pl.BlockSpec(memory_space=pltpu.VMEM)] * (2 + len(arrays)),
        out_specs=[
            pl.BlockSpec((2, TILE, SPAN), lambda g: (g, 0, 0)),
            pl.BlockSpec((4 * TILE, 8, 128), lambda g: (0, g, 0)),
        ],
        scratch_shapes=[
            pltpu.VMEM((8, SPAN, TILE), BF16),
            pltpu.VMEM((8, SPAN, TILE), BF16),
            pltpu.VMEM((8, 6, 1, TILE), F32),
            pltpu.VMEM((8, 1, TILE), F32),
            pltpu.VMEM((4 * TILE, D0), BF16),
            pltpu.VMEM((7, 4 * TILE, 128), F32),
            pltpu.VMEM((4 * TILE, SPAN), BF16),
            pltpu.VMEM((4 * TILE, SPAN), BF16),
            pltpu.VMEM((4 * TILE, SPAN), F32),
        ] + [pltpu.VMEM((SPAN, TILE), F32)] * 4 + [pltpu.VMEM((SPAN, TILE), BF16)] * 4,
        compiler_params=pltpu.CompilerParams(vmem_limit_bytes=60 * 2**20),
        name="main",
    )(order, row_inputs, column_inputs, *arrays)
    return factor, trailing


def exchange(block, axes, groups):
    return lax.all_to_all(block, axes, 0, 0, tiled=True, axis_index_groups=groups)


def per_device(inputs, panel_order):
    own = inputs[:, 0]
    row_count = lax.axis_size("row")
    column_count = lax.axis_size("col")
    turn = [
        (r * column_count + c, (column_count * (r // column_count) + c) * column_count + r % column_count)
        for r in range(row_count) for c in range(column_count)
    ]
    turned = lax.ppermute(own, ("row", "col"), turn)
    row_inputs = lax.all_gather(own, "col", axis=0)
    swap = [(c, c ^ 1) for c in range(column_count)]
    sent = call_small(choose_kernel, panel_order, own, "choose")
    came = exchange(sent, "row", None)
    came, turned = lax.optimization_barrier((came, turned))
    column_inputs = lax.all_gather(turned, "row", axis=0).reshape(2, 8, 4, 32, D0)
    piece = call_small(pick_kernel, panel_order, came, "pick")
    groups = [
        [(z * 4 + y) * column_count + 2 * x + core for y in range(4) for x in range(4)]
        for z in range(row_count // 4) for core in range(2)
    ]
    mine = exchange(piece, ("row", "col"), groups)
    other = lax.ppermute(mine, "col", swap)
    pivot = call_pivot(mine, other)
    factor, trailing = call_main(panel_order, row_inputs, column_inputs, pivot)
    return factor.reshape(4, 1, TILE, SPAN), trailing.reshape(4, 1, TILE, 8, 1, TILE)


def solution(mesh):
    in_specs = (P(None, "row", "col", None), P())
    out_specs = (P(None, "row", None, None), P(None, "row", None, None, "col", None))
    return jax.shard_map(
        per_device, mesh=mesh, in_specs=in_specs, out_specs=out_specs, check_vma=False
    )
```

```python
import math

import jax
import jax.numpy as jnp
from jax import lax
from jax.experimental import pallas as pl
from jax.experimental.pallas import tpu as pltpu
from jax.sharding import PartitionSpec as P

D0 = 768
TILE = 256
PANELS = 2
SPAN = PANELS * TILE
BLOCK = 128
PIVOTS = 8
BIAS = 0.1
RIDGE = 0.1
TINY = 1e-30
EXACT = lax.Precision.HIGHEST
F32 = jnp.float32
BF16 = jnp.bfloat16

ARC = (
    0.30011410855430565,
    0.014911524637152361,
    0.0027575196411184027,
    4.221988638112521e-06,
    0.0005224396428474578,
)


def matmul(left, right, left_dim, right_dim, precision=None):
    return lax.dot_general(
        left, right, (((left_dim,), (right_dim,)), ((), ())), precision=precision,
        preferred_element_type=F32,
    )


def split(value):
    high = value.astype(BF16)
    return high, (value - high.astype(F32)).astype(BF16)


def arc_term(gap):
    series = ARC[4] * gap + ARC[3]
    for coefficient in ARC[2::-1]:
        series = series * gap + coefficient
    return gap * gap * lax.rsqrt(gap) * series


def scales(squares):
    d0 = squares * (1.0 / D0)
    d1 = d0 + BIAS
    d2 = d1 + BIAS
    inverse1 = lax.rsqrt(d1)
    inverse2 = lax.rsqrt(d2)
    root_bias = math.sqrt(BIAS)
    return (
        lax.rsqrt(squares),
        root_bias * inverse1,
        jnp.sqrt(d0) * inverse1,
        root_bias * inverse2,
        jnp.sqrt(d1) * inverse2,
        jnp.sqrt(d2),
    )


def layers(product, rows, columns):
    cosine = product * rows[0] * columns[0]
    gap = jnp.maximum(1.0 - jnp.abs(cosine), TINY)
    value = jnp.maximum(cosine, 0.0) + arc_term(gap)
    for layer in (1, 3):
        gap = 1.0 - rows[layer] * columns[layer]
        gap = jnp.maximum(gap - rows[layer + 1] * columns[layer + 1] * value, TINY)
        value = (1.0 - gap) + arc_term(gap)
    return rows[5] * columns[5] * value


def row_squares(block):
    wide = block.astype(F32)
    return jnp.sum(wide * wide, axis=1, keepdims=True)


def column_squares(block):
    wide = block.astype(F32)
    high, low = split(wide * wide)
    ones = jnp.ones((16, D0), BF16)
    return (matmul(ones, high, 1, 1) + matmul(ones, low, 1, 1))[0:1]


def unit(shape):
    return lax.broadcasted_iota(jnp.int32, shape, 0) == lax.broadcasted_iota(jnp.int32, shape, 1)


def store_scales(squares, out):
    for index, vector in enumerate(scales(squares)):
        out[index] = jnp.broadcast_to(vector, out.shape[1:])


def factor_block(block):
    count = BLOCK // 8
    nb = PIVOTS
    lane = lax.broadcasted_iota(jnp.int32, (8, BLOCK), 1)
    sub = lax.broadcasted_iota(jnp.int32, (8, BLOCK), 0)
    block = list(block)
    inverse = [jnp.where(lane == sub + 8 * g, 1.0, 0.0).astype(F32) for g in range(count)]

    def spread(value):
        return jnp.broadcast_to(value, (8, BLOCK))

    for k in range(0, BLOCK, nb):
        g0, s = k // 8, k % 8
        groups = range(g0 + 1 if s + nb == 8 else g0, count)
        columns = [[None] * count for _ in range(nb)]
        for j in range(nb):
            for g in range(g0, count):
                columns[j][g] = spread(block[g][:, k + j:k + j + 1])
        left = [spread(block[g0][s + j:s + j + 1, :]) for j in range(nb)]
        right = [spread(inverse[g0][s + j:s + j + 1, :]) for j in range(nb)]
        pivot = {
            (i, j): spread(columns[j][g0][s + i:s + i + 1, :])
            for j in range(nb) for i in range(j, nb)
        }
        reciprocal = []
        lower = {}
        for j in range(nb):
            reciprocal.append(1.0 / pivot[j, j])
            for i in range(j + 1, nb):
                lower[i, j] = pivot[i, j] * reciprocal[j]
            for m in range(j + 1, nb):
                for i in range(m, nb):
                    pivot[i, m] = pivot[i, m] - lower[i, j] * pivot[m, j]
        for i in range(nb):
            for j in range(i):
                left[i] = left[i] - lower[i, j] * left[j]
                right[i] = right[i] - lower[i, j] * right[j]
        for g in groups:
            for i in range(nb):
                for j in range(i):
                    columns[i][g] = columns[i][g] - lower[i, j] * columns[j][g]
        left = [left[i] * reciprocal[i] for i in range(nb)]
        scaled = [right[i] * reciprocal[i] for i in range(nb)]
        for g in groups:
            one, two = block[g], inverse[g]
            for i in range(nb):
                if k + nb < BLOCK:
                    one = one - columns[i][g] * left[i]
                two = two - columns[i][g] * scaled[i]
            if g == g0:
                below = sub >= s + nb
                one = jnp.where(below, one, block[g])
                two = jnp.where(below, two, inverse[g])
            block[g], inverse[g] = one, two
        done = inverse[g0]
        for i in range(nb):
            done = jnp.where(sub == s + i, right[i] * lax.rsqrt(pivot[i, i]), done)
        inverse[g0] = done
    return inverse


def invert_factor(matrix, inverse):
    count = SPAN // BLOCK
    inverse[...] = jnp.zeros((SPAN, SPAN), F32)
    for index in range(count):
        o = index * BLOCK
        e = o + BLOCK
        slabs = [matrix[o + 8 * g:o + 8 * g + 8, o:e] for g in range(BLOCK // 8)]
        own = jnp.concatenate(factor_block(slabs), axis=0)
        if index > 0:
            inverse[o:e, 0:o] = matmul(own, inverse[o:e, 0:o], 1, 0, EXACT)
        inverse[o:e, o:e] = own
        if index < count - 1:
            upper = matmul(own, matrix[o:e, e:SPAN], 1, 0, EXACT)
            matrix[e:SPAN, e:SPAN] -= matmul(upper, upper, 0, 0, EXACT)
            inverse[e:SPAN, 0:e] -= matmul(upper, inverse[o:e, 0:e], 0, 0, EXACT)


def choose_kernel(order, own, out):
    for k in range(PANELS):
        rows = own[order[k] // 16].astype(F32)
        for device in range(16):
            start = device % 4 * 8
            out[device, k] = rows[start:start + 8].astype(BF16)


def pick_kernel(order, came, out):
    for k in range(PANELS):
        rows = came[order[k] % 16, k]
        for device in range(16):
            out[device, k] = rows


def pivot_kernel(mine, other, panel, high_out, low_out, mean_out, mean_row_out, center_out, center_row_out,
                 scales_out, scales_row_out, matrix, inverse):
    core = lax.axis_index("col") % 2
    for source, side in ((mine, core), (other, 1 - core)):
        for k in range(PANELS):
            for x in range(4):
                for y in (0, 2):
                    rows = [source[(y + i) * 4 + x, k].astype(F32) for i in range(2)]
                    start = pl.multiple_of(k * TILE + 64 * x + 32 * side + 8 * y, 16)
                    panel[pl.ds(start, 16), :] = jnp.concatenate(rows, axis=0).astype(BF16)
    store_scales(row_squares(panel[...]), scales_out)
    for index, vector in enumerate(scales(column_squares(panel[...]))):
        scales_row_out[index] = vector
    for index in range(4):
        rows = slice(index * BLOCK, (index + 1) * BLOCK)
        product = matmul(panel[rows, :], panel[...], 1, 1)
        for lanes in range(4):
            columns = slice(lanes * BLOCK, (lanes + 1) * BLOCK)
            matrix[rows, columns] = BIAS + layers(
                product[:, columns],
                [scales_out[i, rows] for i in range(6)],
                [scales_row_out[i, :, columns] for i in range(6)],
            )
    mean_row = jnp.sum(matrix[...], axis=0, keepdims=True) * (1.0 / SPAN)
    mean_row_out[...] = mean_row
    mean = jnp.sum(matrix[...], axis=1, keepdims=True) * (1.0 / SPAN)
    mean_out[...] = jnp.broadcast_to(mean, mean_out.shape)
    matrix[...] += jnp.where(unit((SPAN, SPAN)), RIDGE, 0.0)
    invert_factor(matrix, inverse)
    high, low = split(inverse[...])
    high_out[...] = high
    low_out[...] = low
    center = jnp.sum(inverse[...] * mean_row, axis=1, keepdims=True)
    center_out[...] = jnp.broadcast_to(center, center_out.shape)
    center_row_out[...] = matmul(
        jnp.broadcast_to(mean_row, (8, SPAN)), inverse[...], 1, 1, EXACT
    )[0:1]


def eye_term(start, lanes, amount):
    row = lax.broadcasted_iota(jnp.int32, (64, 128), 0) + (start - lanes)
    return jnp.where(row == lax.broadcasted_iota(jnp.int32, (64, 128), 1), amount, 0.0)


def main_kernel(order, row0, row1, row2, row3, turn0, turn1, turn2, turn3, column_inputs, panel,
                high_in, low_in, mean, mean_row, center, center_row, panel_scales,
                panel_scales_row, factor_out, trailing_out,
                column_high, column_low, column_scales, column_shift,
                own, row_scales, row_high, row_low, row_factor,
                product0, product1, update0, update1, high0, high1, low0, low1):
    group = pl.program_id(0)
    row_position, column_position = lax.axis_index("row"), lax.axis_index("col")
    product, update = (product0, product1), (update0, update1)
    panel_high, panel_low = (high0, high1), (low0, low1)

    def column_block(p):
        return column_inputs[p % 2, :, p // 2].reshape(TILE, D0)

    def ridge_of(tile, index):
        return jnp.where(order[index] == tile, RIDGE, 0.0).astype(F32)

    def column_first(p, slot):
        block = column_block(p)
        product[slot][...] = matmul(panel[...], block, 1, 1)
        for index, vector in enumerate(scales(column_squares(block))):
            column_scales[p, index] = vector

    def column_middle(p, slot):
        for start in range(0, SPAN, 64):
            index = start // TILE
            ridge = ridge_of(p * 8 + column_position, index)
            rows = slice(start, start + 64)
            for lanes in (0, 128):
                wide = slice(lanes, lanes + 128)
                value = (BIAS - mean[rows]) + layers(
                    product[slot][rows, wide],
                    [panel_scales[i, rows] for i in range(6)],
                    [column_scales[p, i, :, wide] for i in range(6)],
                )
                if start % TILE // 128 * 128 == lanes:
                    value = value + eye_term(start % TILE, lanes, ridge)
                high, low = split(value)
                panel_high[slot][rows, wide] = high
                panel_low[slot][rows, wide] = low

    def column_last(p, slot):
        shift = 0.0
        for index in range(PANELS):
            rows = slice(index * TILE, (index + 1) * TILE)
            depth = (index + 1) * TILE
            high, low = panel_high[slot][:depth, :], panel_low[slot][:depth, :]
            factor = matmul(high_in[rows, :depth], high, 1, 0) + (
                matmul(high_in[rows, :depth], low, 1, 0) + matmul(low_in[rows, :depth], high, 1, 0)
            )
            weight = center[rows]
            shift = shift + jnp.sum(
                factor * jnp.concatenate([weight, weight], axis=1), axis=0, keepdims=True
            )
            high, low = split(factor)
            column_high[p, rows] = high
            column_low[p, rows] = low
        column_shift[p] = shift

    def row_first(q, slot):
        block = own[pl.ds(pl.multiple_of(q * TILE, TILE), TILE), :]
        for index in range(PANELS):
            rows = slice(index * TILE, (index + 1) * TILE)
            product[slot][rows, :] = matmul(block, panel[rows, :], 1, 1)

    def row_middle(q, slot):
        for index in range(PANELS):
            ridge = ridge_of(q * 16 + row_position, index)
            for start in range(0, TILE, 64):
                rows = pl.ds(pl.multiple_of(q * TILE + start, 64), 64)
                here = slice(index * TILE + start, index * TILE + start + 64)
                for lanes in (0, 128):
                    wide = slice(index * TILE + lanes, index * TILE + lanes + 128)
                    value = (BIAS - mean_row[:, wide]) + layers(
                        product[slot][here, lanes:lanes + 128],
                        [row_scales[i, rows] for i in range(6)],
                        [panel_scales_row[i, :, wide] for i in range(6)],
                    )
                    if start // 128 * 128 == lanes:
                        value = value + eye_term(start, lanes, ridge)
                    high, low = split(value)
                    panel_high[slot][here, lanes:lanes + 128] = high
                    panel_low[slot][here, lanes:lanes + 128] = low

    def row_last(q, slot):
        rows = pl.ds(pl.multiple_of(q * TILE, TILE), TILE)
        shift = BIAS - jnp.sum(center_row[...] * center_row[...], axis=1, keepdims=True)
        for index in range(PANELS):
            wide = slice(index * TILE, (index + 1) * TILE)
            factor = 0.0
            for part in range(index + 1):
                depth = slice(part * TILE, (part + 1) * TILE)
                high, low = panel_high[slot][depth, :], panel_low[slot][depth, :]
                factor = factor + (
                    matmul(high, high_in[wide, depth], 1, 1)
                    + (matmul(high, low_in[wide, depth], 1, 1) + matmul(low, high_in[wide, depth], 1, 1))
                )
            row_factor[rows, wide] = factor + center_row[:, wide]
            shift = shift - jnp.sum(factor * center_row[:, wide], axis=1, keepdims=True)
            high, low = split(factor)
            row_high[rows, wide] = high
            row_low[rows, wide] = low
        row_scales[6, rows] = jnp.broadcast_to(shift, (TILE, 128))

    def pipeline(count, first, middle, last):
        first(0, 0)

        def pair(step, _):
            for slot in range(2):
                at = step * 2 + slot
                last(jnp.maximum(at - 1, 0), 1 - slot)
                first(jnp.minimum(at + 1, count - 1), 1 - slot)
                middle(at, slot)
            return 0

        lax.fori_loop(0, count // 2, pair, 0)
        last(count - 1, 1)

    @pl.when(group == 0)
    def _():
        core = column_position % 2
        sides = (((row0, row1, row2, row3), core), ((turn0, turn1, turn2, turn3), 1 - core))
        for sources, side in sides:
            for step, source in enumerate(sources):
                chip = (column_position // 2 + 4 - step) % 4
                for q in range(4):
                    start = pl.multiple_of(q * TILE + (chip * 2 + side) * 32, 32)
                    own[pl.ds(start, 32), :] = source[q]
        for start in range(0, 4 * TILE, 128):
            for index, vector in enumerate(scales(row_squares(own[start:start + 128, :]))):
                row_scales[index, start:start + 128] = jnp.broadcast_to(vector, (128, 128))
        pipeline(4, row_first, row_middle, row_last)
        pipeline(8, column_first, column_middle, column_last)

    for half in range(2):
        rows = pl.ds(pl.multiple_of(group * 2 * TILE + half * TILE, TILE), TILE)
        factor_out[half] = row_factor[rows, :]

    def tile_first(p, slot):
        rows = slice(slot * SPAN, (slot + 1) * SPAN)
        product[slot][...] = matmul(own[rows, :], column_block(p), 1, 1)
        update[slot][...] = matmul(row_high[rows, :], column_high[p], 1, 0) + (
            matmul(row_high[rows, :], column_low[p], 1, 0)
            + matmul(row_low[rows, :], column_high[p], 1, 0)
        )

    def tile_middle(p, slot):
        for start in range(0, SPAN, 64):
            here = slice(start, start + 64)
            rows = slice(slot * SPAN + start, slot * SPAN + start + 64)
            for half in range(2):
                wide = slice(half * 128, half * 128 + 128)
                value = layers(
                    product[slot][here, wide],
                    [row_scales[i, rows] for i in range(6)],
                    [column_scales[p, i, :, wide] for i in range(6)],
                )
                value = value + (row_scales[6, rows] - column_shift[p, :, wide])
                value = value - update[slot][here, wide]
                at = (slot * SPAN + start) * 8 + p % 4 * 2 + half
                trailing[pl.ds(at, 64, stride=8), :] = value

    trailing = trailing_out.reshape(4 * TILE * 8, 128)
    tile_first(group * 4, 0)

    def tile(step, _):
        p = group * 4 + step
        tile_first(p, 1)
        tile_middle(p, 0)
        tile_first(jnp.minimum(p + 1, 7), 0)
        tile_middle(p, 1)
        return 0

    lax.fori_loop(0, 4, tile, 0)

    @pl.when(row_position % 8 == column_position)
    def _():
        for part in range(2):
            q = group * 2 + part
            p = part * 2 + row_position // 8
            for start in range(0, TILE, 64):
                half = start // 128
                at = pl.ds(pl.multiple_of(q * TILE + start, 64), 64)
                trailing_out[at, p * 2 + half, :] += eye_term(start, half * 128, RIDGE)


def whole(shape):
    return pl.BlockSpec(shape, lambda *_: (0,) * len(shape))


def call_small(kernel, order, block, name):
    return pl.pallas_call(
        kernel,
        out_shape=jax.ShapeDtypeStruct((16, PANELS, 8, D0), BF16),
        in_specs=[pl.BlockSpec(memory_space=pltpu.SMEM), pl.BlockSpec(memory_space=pltpu.VMEM)],
        name=name,
    )(order, block)


def call_pivot(mine, other):
    shapes = [
        ((SPAN, D0), BF16),
        ((SPAN, SPAN), BF16), ((SPAN, SPAN), BF16), ((SPAN, 128), F32), ((1, SPAN), F32),
        ((SPAN, 128), F32), ((1, SPAN), F32), ((6, SPAN, 128), F32), ((6, 1, SPAN), F32),
    ]
    return pl.pallas_call(
        pivot_kernel,
        out_shape=[jax.ShapeDtypeStruct(s, d) for s, d in shapes],
        in_specs=[pl.BlockSpec(memory_space=pltpu.VMEM)] * 2,
        scratch_shapes=[pltpu.VMEM((SPAN, SPAN), F32), pltpu.VMEM((SPAN, SPAN), F32)],
        compiler_params=pltpu.CompilerParams(vmem_limit_bytes=60 * 2**20),
        cost_estimate=pl.CostEstimate(flops=3 * 10**10, bytes_accessed=4 * 10**6, transcendentals=0),
        name="pivot",
    )(mine, other)


def call_main(order, row_inputs, column_inputs, arrays):
    factor, trailing = pl.pallas_call(
        main_kernel,
        grid=(2,),
        out_shape=[
            jax.ShapeDtypeStruct((4, TILE, SPAN), F32),
            jax.ShapeDtypeStruct((4 * TILE, 16, 128), F32),
        ],
        in_specs=[pl.BlockSpec(memory_space=pltpu.SMEM)]
        + [pl.BlockSpec(memory_space=pltpu.VMEM)] * (9 + len(arrays)),
        out_specs=[
            pl.BlockSpec((2, TILE, SPAN), lambda g: (g, 0, 0)),
            pl.BlockSpec((4 * TILE, 8, 128), lambda g: (0, g, 0)),
        ],
        scratch_shapes=[
            pltpu.VMEM((8, SPAN, TILE), BF16),
            pltpu.VMEM((8, SPAN, TILE), BF16),
            pltpu.VMEM((8, 6, 1, TILE), F32),
            pltpu.VMEM((8, 1, TILE), F32),
            pltpu.VMEM((4 * TILE, D0), BF16),
            pltpu.VMEM((7, 4 * TILE, 128), F32),
            pltpu.VMEM((4 * TILE, SPAN), BF16),
            pltpu.VMEM((4 * TILE, SPAN), BF16),
            pltpu.VMEM((4 * TILE, SPAN), F32),
        ] + [pltpu.VMEM((SPAN, TILE), F32)] * 4 + [pltpu.VMEM((SPAN, TILE), BF16)] * 4,
        compiler_params=pltpu.CompilerParams(vmem_limit_bytes=60 * 2**20),
        name="main",
    )(order, *row_inputs, column_inputs, *arrays)
    return factor, trailing


def exchange(block, axes, groups):
    return lax.all_to_all(block, axes, 0, 0, tiled=True, axis_index_groups=groups)


def per_device(inputs, panel_order):
    own = inputs[:, 0]
    row_count = lax.axis_size("row")
    column_count = lax.axis_size("col")
    turn = [
        (r * column_count + c, (column_count * (r // column_count) + c) * column_count + r % column_count)
        for r in range(row_count) for c in range(column_count)
    ]
    turned = lax.ppermute(own, ("row", "col"), turn)
    swap = [(c, c ^ 1) for c in range(column_count)]
    row_inputs = [own] + [
        lax.ppermute(own, "col", [(c, (c + 2 * step) % column_count) for c in range(column_count)])
        for step in range(1, 4)
    ]
    sent = call_small(choose_kernel, panel_order, own, "choose")
    came = exchange(sent, "row", None)
    came, turned = lax.optimization_barrier((came, turned))
    column_inputs = lax.all_gather(turned, "row", axis=0).reshape(2, 8, 4, 32, D0)
    piece = call_small(pick_kernel, panel_order, came, "pick")
    groups = [
        [(z * 4 + y) * column_count + 2 * x + core for y in range(4) for x in range(4)]
        for z in range(row_count // 4) for core in range(2)
    ]
    mine = exchange(piece, ("row", "col"), groups)
    other = lax.ppermute(mine, "col", swap)
    pivot = call_pivot(mine, other)
    first, *row_inputs = lax.optimization_barrier((pivot[0], *row_inputs))
    pivot = (first, *pivot[1:])
    row_inputs += [lax.ppermute(block, "col", swap) for block in row_inputs]
    factor, trailing = call_main(panel_order, row_inputs, column_inputs, pivot)
    return factor.reshape(4, 1, TILE, SPAN), trailing.reshape(4, 1, TILE, 8, 1, TILE)


def solution(mesh):
    in_specs = (P(None, "row", "col", None), P())
    out_specs = (P(None, "row", None, None), P(None, "row", None, None, "col", None))
    return jax.shard_map(
        per_device, mesh=mesh, in_specs=in_specs, out_specs=out_specs, check_vma=False
    )
```

```python
import math

import jax
import jax.numpy as jnp
from jax import lax
from jax.experimental import pallas as pl
from jax.experimental.pallas import tpu as pltpu
from jax.sharding import PartitionSpec as P

D0 = 768
TILE = 256
PANELS = 2
SPAN = PANELS * TILE
BLOCK = 128
PIVOTS = 8
BIAS = 0.1
RIDGE = 0.1
TINY = 1e-30
EXACT = lax.Precision.HIGHEST
F32 = jnp.float32
BF16 = jnp.bfloat16

ARC = (
    0.30011410855430565,
    0.014911524637152361,
    0.0027575196411184027,
    4.221988638112521e-06,
    0.0005224396428474578,
)


def matmul(left, right, left_dim, right_dim, precision=None):
    return lax.dot_general(
        left, right, (((left_dim,), (right_dim,)), ((), ())), precision=precision,
        preferred_element_type=F32,
    )


def split(value):
    high = value.astype(BF16)
    return high, (value - high.astype(F32)).astype(BF16)


def arc_term(gap):
    series = ARC[4] * gap + ARC[3]
    for coefficient in ARC[2::-1]:
        series = series * gap + coefficient
    return gap * gap * lax.rsqrt(gap) * series


def scales(squares):
    d0 = squares * (1.0 / D0)
    d1 = d0 + BIAS
    d2 = d1 + BIAS
    inverse1 = lax.rsqrt(d1)
    inverse2 = lax.rsqrt(d2)
    root_bias = math.sqrt(BIAS)
    return (
        lax.rsqrt(squares),
        root_bias * inverse1,
        jnp.sqrt(d0) * inverse1,
        root_bias * inverse2,
        jnp.sqrt(d1) * inverse2,
        jnp.sqrt(d2),
    )


def layers(product, rows, columns):
    cosine = product * rows[0] * columns[0]
    gap = jnp.maximum(1.0 - jnp.abs(cosine), TINY)
    value = jnp.maximum(cosine, 0.0) + arc_term(gap)
    for layer in (1, 3):
        gap = 1.0 - rows[layer] * columns[layer]
        gap = jnp.maximum(gap - rows[layer + 1] * columns[layer + 1] * value, TINY)
        value = (1.0 - gap) + arc_term(gap)
    return rows[5] * columns[5] * value


def row_squares(block):
    wide = block.astype(F32)
    return jnp.sum(wide * wide, axis=1, keepdims=True)


def column_squares(block):
    return jnp.transpose(jnp.broadcast_to(row_squares(block), (block.shape[0], 128)))[0:1]


def unit(shape):
    return lax.broadcasted_iota(jnp.int32, shape, 0) == lax.broadcasted_iota(jnp.int32, shape, 1)


def store_scales(squares, out):
    for index, vector in enumerate(scales(squares)):
        out[index] = jnp.broadcast_to(vector, out.shape[1:])


def factor_block(block):
    count = BLOCK // 8
    nb = PIVOTS
    lane = lax.broadcasted_iota(jnp.int32, (8, BLOCK), 1)
    sub = lax.broadcasted_iota(jnp.int32, (8, BLOCK), 0)
    block = list(block)
    inverse = [jnp.where(lane == sub + 8 * g, 1.0, 0.0).astype(F32) for g in range(count)]

    def spread(value):
        return jnp.broadcast_to(value, (8, BLOCK))

    for k in range(0, BLOCK, nb):
        g0, s = k // 8, k % 8
        groups = range(g0 + 1 if s + nb == 8 else g0, count)
        columns = [[None] * count for _ in range(nb)]
        for j in range(nb):
            for g in range(g0, count):
                columns[j][g] = spread(block[g][:, k + j:k + j + 1])
        left = [spread(block[g0][s + j:s + j + 1, :]) for j in range(nb)]
        right = [spread(inverse[g0][s + j:s + j + 1, :]) for j in range(nb)]
        pivot = {
            (i, j): spread(columns[j][g0][s + i:s + i + 1, :])
            for j in range(nb) for i in range(j, nb)
        }
        reciprocal = []
        lower = {}
        for j in range(nb):
            reciprocal.append(1.0 / pivot[j, j])
            for i in range(j + 1, nb):
                lower[i, j] = pivot[i, j] * reciprocal[j]
            for m in range(j + 1, nb):
                for i in range(m, nb):
                    pivot[i, m] = pivot[i, m] - lower[i, j] * pivot[m, j]
        for i in range(nb):
            for j in range(i):
                left[i] = left[i] - lower[i, j] * left[j]
                right[i] = right[i] - lower[i, j] * right[j]
        for g in groups:
            for i in range(nb):
                for j in range(i):
                    columns[i][g] = columns[i][g] - lower[i, j] * columns[j][g]
        left = [left[i] * reciprocal[i] for i in range(nb)]
        scaled = [right[i] * reciprocal[i] for i in range(nb)]
        for g in groups:
            one, two = block[g], inverse[g]
            for i in range(nb):
                if k + nb < BLOCK:
                    one = one - columns[i][g] * left[i]
                two = two - columns[i][g] * scaled[i]
            if g == g0:
                below = sub >= s + nb
                one = jnp.where(below, one, block[g])
                two = jnp.where(below, two, inverse[g])
            block[g], inverse[g] = one, two
        done = inverse[g0]
        for i in range(nb):
            done = jnp.where(sub == s + i, right[i] * lax.rsqrt(pivot[i, i]), done)
        inverse[g0] = done
    return inverse


def invert_factor(matrix, inverse):
    count = SPAN // BLOCK
    inverse[...] = jnp.zeros((SPAN, SPAN), F32)
    for index in range(count):
        o = index * BLOCK
        e = o + BLOCK
        slabs = [matrix[o + 8 * g:o + 8 * g + 8, o:e] for g in range(BLOCK // 8)]
        own = jnp.concatenate(factor_block(slabs), axis=0)
        if index > 0:
            inverse[o:e, 0:o] = matmul(own, inverse[o:e, 0:o], 1, 0, EXACT)
        inverse[o:e, o:e] = own
        if index < count - 1:
            upper = matmul(own, matrix[o:e, e:SPAN], 1, 0, EXACT)
            matrix[e:SPAN, e:SPAN] -= matmul(upper, upper, 0, 0, EXACT)
            inverse[e:SPAN, 0:e] -= matmul(upper, inverse[o:e, 0:e], 0, 0, EXACT)


def choose_kernel(order, own, out):
    for k in range(PANELS):
        rows = own[order[k] // 16].astype(F32)
        for device in range(16):
            start = device % 4 * 8
            out[device, k] = rows[start:start + 8].astype(BF16)


def pick_kernel(order, came, out):
    for k in range(PANELS):
        rows = came[order[k] % 16, k]
        for device in range(16):
            out[device, k] = rows


def pivot_kernel(mine, other, panel, high_out, low_out, mean_out, mean_row_out, center_out, center_row_out,
                 scales_out, scales_row_out, matrix, inverse):
    core = lax.axis_index("col") % 2
    for source, side in ((mine, core), (other, 1 - core)):
        for k in range(PANELS):
            for x in range(4):
                for y in (0, 2):
                    rows = [source[(y + i) * 4 + x, k].astype(F32) for i in range(2)]
                    start = pl.multiple_of(k * TILE + 64 * x + 32 * side + 8 * y, 16)
                    panel[pl.ds(start, 16), :] = jnp.concatenate(rows, axis=0).astype(BF16)
    store_scales(row_squares(panel[...]), scales_out)
    for index, vector in enumerate(scales(column_squares(panel[...]))):
        scales_row_out[index] = vector
    for index in range(4):
        rows = slice(index * BLOCK, (index + 1) * BLOCK)
        product = matmul(panel[rows, :], panel[...], 1, 1)
        for lanes in range(4):
            columns = slice(lanes * BLOCK, (lanes + 1) * BLOCK)
            matrix[rows, columns] = BIAS + layers(
                product[:, columns],
                [scales_out[i, rows] for i in range(6)],
                [scales_row_out[i, :, columns] for i in range(6)],
            )
    mean_row = jnp.sum(matrix[...], axis=0, keepdims=True) * (1.0 / SPAN)
    mean_row_out[...] = mean_row
    mean = jnp.sum(matrix[...], axis=1, keepdims=True) * (1.0 / SPAN)
    mean_out[...] = jnp.broadcast_to(mean, mean_out.shape)
    matrix[...] += jnp.where(unit((SPAN, SPAN)), RIDGE, 0.0)
    invert_factor(matrix, inverse)
    high, low = split(inverse[...])
    high_out[...] = high
    low_out[...] = low
    center = jnp.sum(inverse[...] * mean_row, axis=1, keepdims=True)
    center_out[...] = jnp.broadcast_to(center, center_out.shape)
    center_row_out[...] = matmul(
        jnp.broadcast_to(mean_row, (8, SPAN)), inverse[...], 1, 1, EXACT
    )[0:1]


def eye_term(start, lanes, amount):
    row = lax.broadcasted_iota(jnp.int32, (64, 128), 0) + (start - lanes)
    return jnp.where(row == lax.broadcasted_iota(jnp.int32, (64, 128), 1), amount, 0.0)


def main_kernel(order, row0, row1, row2, row3, turn0, turn1, turn2, turn3, column_inputs, panel,
                high_in, low_in, mean, mean_row, center, center_row, panel_scales,
                panel_scales_row, factor_out, trailing_out,
                column_high, column_low, column_scales, column_shift,
                own, row_scales, row_high, row_low, row_factor,
                product0, product1, update0, update1, high0, high1, low0, low1):
    group = pl.program_id(0)
    row_position, column_position = lax.axis_index("row"), lax.axis_index("col")
    product, update = (product0, product1), (update0, update1)
    panel_high, panel_low = (high0, high1), (low0, low1)

    def column_block(p):
        return column_inputs[p % 2, :, p // 2].reshape(TILE, D0)

    def ridge_of(tile, index):
        return jnp.where(order[index] == tile, RIDGE, 0.0).astype(F32)

    def column_first(p, slot):
        block = column_block(p)
        product[slot][...] = matmul(panel[...], block, 1, 1)
        for index, vector in enumerate(scales(column_squares(block))):
            column_scales[p, index] = vector

    def column_middle(p, slot):
        for start in range(0, SPAN, 64):
            index = start // TILE
            ridge = ridge_of(p * 8 + column_position, index)
            rows = slice(start, start + 64)
            for lanes in (0, 128):
                wide = slice(lanes, lanes + 128)
                value = (BIAS - mean[rows]) + layers(
                    product[slot][rows, wide],
                    [panel_scales[i, rows] for i in range(6)],
                    [column_scales[p, i, :, wide] for i in range(6)],
                )
                if start % TILE // 128 * 128 == lanes:
                    value = value + eye_term(start % TILE, lanes, ridge)
                high, low = split(value)
                panel_high[slot][rows, wide] = high
                panel_low[slot][rows, wide] = low

    def column_last(p, slot):
        shift = 0.0
        for index in range(PANELS):
            rows = slice(index * TILE, (index + 1) * TILE)
            depth = (index + 1) * TILE
            high, low = panel_high[slot][:depth, :], panel_low[slot][:depth, :]
            factor = matmul(high_in[rows, :depth], high, 1, 0) + (
                matmul(high_in[rows, :depth], low, 1, 0) + matmul(low_in[rows, :depth], high, 1, 0)
            )
            weight = center[rows]
            shift = shift + jnp.sum(
                factor * jnp.concatenate([weight, weight], axis=1), axis=0, keepdims=True
            )
            high, low = split(factor)
            column_high[p, rows] = high
            column_low[p, rows] = low
        column_shift[p] = shift

    def row_first(q, slot):
        block = own[pl.ds(pl.multiple_of(q * TILE, TILE), TILE), :]
        for index in range(PANELS):
            rows = slice(index * TILE, (index + 1) * TILE)
            product[slot][rows, :] = matmul(block, panel[rows, :], 1, 1)

    def row_middle(q, slot):
        for index in range(PANELS):
            ridge = ridge_of(q * 16 + row_position, index)
            for start in range(0, TILE, 64):
                rows = pl.ds(pl.multiple_of(q * TILE + start, 64), 64)
                here = slice(index * TILE + start, index * TILE + start + 64)
                for lanes in (0, 128):
                    wide = slice(index * TILE + lanes, index * TILE + lanes + 128)
                    value = (BIAS - mean_row[:, wide]) + layers(
                        product[slot][here, lanes:lanes + 128],
                        [row_scales[i, rows] for i in range(6)],
                        [panel_scales_row[i, :, wide] for i in range(6)],
                    )
                    if start // 128 * 128 == lanes:
                        value = value + eye_term(start, lanes, ridge)
                    high, low = split(value)
                    panel_high[slot][here, lanes:lanes + 128] = high
                    panel_low[slot][here, lanes:lanes + 128] = low

    def row_last(q, slot):
        rows = pl.ds(pl.multiple_of(q * TILE, TILE), TILE)
        shift = BIAS - jnp.sum(center_row[...] * center_row[...], axis=1, keepdims=True)
        for index in range(PANELS):
            wide = slice(index * TILE, (index + 1) * TILE)
            factor = 0.0
            for part in range(index + 1):
                depth = slice(part * TILE, (part + 1) * TILE)
                high, low = panel_high[slot][depth, :], panel_low[slot][depth, :]
                factor = factor + (
                    matmul(high, high_in[wide, depth], 1, 1)
                    + (matmul(high, low_in[wide, depth], 1, 1) + matmul(low, high_in[wide, depth], 1, 1))
                )
            row_factor[rows, wide] = factor + center_row[:, wide]
            shift = shift - jnp.sum(factor * center_row[:, wide], axis=1, keepdims=True)
            high, low = split(factor)
            row_high[rows, wide] = high
            row_low[rows, wide] = low
        row_scales[6, rows] = jnp.broadcast_to(shift, (TILE, 128))

    def pipeline(count, first, middle, last):
        first(0, 0)

        def pair(step, _):
            for slot in range(2):
                at = step * 2 + slot
                last(jnp.maximum(at - 1, 0), 1 - slot)
                first(jnp.minimum(at + 1, count - 1), 1 - slot)
                middle(at, slot)
            return 0

        lax.fori_loop(0, count // 2, pair, 0)
        last(count - 1, 1)

    @pl.when(group == 0)
    def _():
        core = column_position % 2
        sides = (((row0, row1, row2, row3), core), ((turn0, turn1, turn2, turn3), 1 - core))
        for sources, side in sides:
            for step, source in enumerate(sources):
                chip = (column_position // 2 + 4 - step) % 4
                for q in range(4):
                    start = pl.multiple_of(q * TILE + (chip * 2 + side) * 32, 32)
                    own[pl.ds(start, 32), :] = source[q]
        for start in range(0, 4 * TILE, 128):
            for index, vector in enumerate(scales(row_squares(own[start:start + 128, :]))):
                row_scales[index, start:start + 128] = jnp.broadcast_to(vector, (128, 128))
        pipeline(4, row_first, row_middle, row_last)
        pipeline(8, column_first, column_middle, column_last)

    for half in range(2):
        rows = pl.ds(pl.multiple_of(group * 2 * TILE + half * TILE, TILE), TILE)
        factor_out[half] = row_factor[rows, :]

    def tile_first(p, slot):
        rows = slice(slot * SPAN, (slot + 1) * SPAN)
        product[slot][...] = matmul(own[rows, :], column_block(p), 1, 1)
        update[slot][...] = matmul(row_high[rows, :], column_high[p], 1, 0) + (
            matmul(row_high[rows, :], column_low[p], 1, 0)
            + matmul(row_low[rows, :], column_high[p], 1, 0)
        )

    def tile_middle(p, slot):
        for start in range(0, SPAN, 64):
            here = slice(start, start + 64)
            rows = slice(slot * SPAN + start, slot * SPAN + start + 64)
            for half in range(2):
                wide = slice(half * 128, half * 128 + 128)
                value = layers(
                    product[slot][here, wide],
                    [row_scales[i, rows] for i in range(6)],
                    [column_scales[p, i, :, wide] for i in range(6)],
                )
                value = value + (row_scales[6, rows] - column_shift[p, :, wide])
                value = value - update[slot][here, wide]
                at = (slot * SPAN + start) * 8 + p % 4 * 2 + half
                trailing[pl.ds(at, 64, stride=8), :] = value

    trailing = trailing_out.reshape(4 * TILE * 8, 128)
    tile_first(group * 4, 0)

    def tile(step, _):
        p = group * 4 + step
        tile_first(p, 1)
        tile_middle(p, 0)
        tile_first(jnp.minimum(p + 1, 7), 0)
        tile_middle(p, 1)
        return 0

    lax.fori_loop(0, 4, tile, 0)

    @pl.when(row_position % 8 == column_position)
    def _():
        for part in range(2):
            q = group * 2 + part
            p = part * 2 + row_position // 8
            for start in range(0, TILE, 64):
                half = start // 128
                at = pl.ds(pl.multiple_of(q * TILE + start, 64), 64)
                trailing_out[at, p * 2 + half, :] += eye_term(start, half * 128, RIDGE)


def whole(shape):
    return pl.BlockSpec(shape, lambda *_: (0,) * len(shape))


def call_small(kernel, order, block, name):
    return pl.pallas_call(
        kernel,
        out_shape=jax.ShapeDtypeStruct((16, PANELS, 8, D0), BF16),
        in_specs=[pl.BlockSpec(memory_space=pltpu.SMEM), pl.BlockSpec(memory_space=pltpu.VMEM)],
        name=name,
    )(order, block)


def call_pivot(mine, other):
    shapes = [
        ((SPAN, D0), BF16),
        ((SPAN, SPAN), BF16), ((SPAN, SPAN), BF16), ((SPAN, 128), F32), ((1, SPAN), F32),
        ((SPAN, 128), F32), ((1, SPAN), F32), ((6, SPAN, 128), F32), ((6, 1, SPAN), F32),
    ]
    return pl.pallas_call(
        pivot_kernel,
        out_shape=[jax.ShapeDtypeStruct(s, d) for s, d in shapes],
        in_specs=[pl.BlockSpec(memory_space=pltpu.VMEM)] * 2,
        scratch_shapes=[pltpu.VMEM((SPAN, SPAN), F32), pltpu.VMEM((SPAN, SPAN), F32)],
        compiler_params=pltpu.CompilerParams(vmem_limit_bytes=60 * 2**20),
        cost_estimate=pl.CostEstimate(flops=3 * 10**10, bytes_accessed=4 * 10**6, transcendentals=0),
        name="pivot",
    )(mine, other)


def call_main(order, row_inputs, column_inputs, arrays):
    factor, trailing = pl.pallas_call(
        main_kernel,
        grid=(2,),
        out_shape=[
            jax.ShapeDtypeStruct((4, TILE, SPAN), F32),
            jax.ShapeDtypeStruct((4 * TILE, 16, 128), F32),
        ],
        in_specs=[pl.BlockSpec(memory_space=pltpu.SMEM)]
        + [pl.BlockSpec(memory_space=pltpu.VMEM)] * (9 + len(arrays)),
        out_specs=[
            pl.BlockSpec((2, TILE, SPAN), lambda g: (g, 0, 0)),
            pl.BlockSpec((4 * TILE, 8, 128), lambda g: (0, g, 0)),
        ],
        scratch_shapes=[
            pltpu.VMEM((8, SPAN, TILE), BF16),
            pltpu.VMEM((8, SPAN, TILE), BF16),
            pltpu.VMEM((8, 6, 1, TILE), F32),
            pltpu.VMEM((8, 1, TILE), F32),
            pltpu.VMEM((4 * TILE, D0), BF16),
            pltpu.VMEM((7, 4 * TILE, 128), F32),
            pltpu.VMEM((4 * TILE, SPAN), BF16),
            pltpu.VMEM((4 * TILE, SPAN), BF16),
            pltpu.VMEM((4 * TILE, SPAN), F32),
        ] + [pltpu.VMEM((SPAN, TILE), F32)] * 4 + [pltpu.VMEM((SPAN, TILE), BF16)] * 4,
        compiler_params=pltpu.CompilerParams(vmem_limit_bytes=60 * 2**20),
        name="main",
    )(order, *row_inputs, column_inputs, *arrays)
    return factor, trailing


def exchange(block, axes, groups):
    return lax.all_to_all(block, axes, 0, 0, tiled=True, axis_index_groups=groups)


def per_device(inputs, panel_order):
    own = inputs[:, 0]
    row_count = lax.axis_size("row")
    column_count = lax.axis_size("col")
    turn = [
        (r * column_count + c, (column_count * (r // column_count) + c) * column_count + r % column_count)
        for r in range(row_count) for c in range(column_count)
    ]
    turned = lax.ppermute(own, ("row", "col"), turn)
    swap = [(c, c ^ 1) for c in range(column_count)]
    row_inputs = [own] + [
        lax.ppermute(own, "col", [(c, (c + 2 * step) % column_count) for c in range(column_count)])
        for step in range(1, 4)
    ]
    sent = call_small(choose_kernel, panel_order, own, "choose")
    came = exchange(sent, "row", None)
    came, turned = lax.optimization_barrier((came, turned))
    column_inputs = lax.all_gather(turned, "row", axis=0).reshape(2, 8, 4, 32, D0)
    piece = call_small(pick_kernel, panel_order, came, "pick")
    groups = [
        [(z * 4 + y) * column_count + 2 * x + core for y in range(4) for x in range(4)]
        for z in range(row_count // 4) for core in range(2)
    ]
    mine = exchange(piece, ("row", "col"), groups)
    other = lax.ppermute(mine, "col", swap)
    pivot = call_pivot(mine, other)
    first, *row_inputs = lax.optimization_barrier((pivot[0], *row_inputs))
    pivot = (first, *pivot[1:])
    row_inputs += [lax.ppermute(block, "col", swap) for block in row_inputs]
    factor, trailing = call_main(panel_order, row_inputs, column_inputs, pivot)
    return factor.reshape(4, 1, TILE, SPAN), trailing.reshape(4, 1, TILE, 8, 1, TILE)


def solution(mesh):
    in_specs = (P(None, "row", "col", None), P())
    out_specs = (P(None, "row", None, None), P(None, "row", None, None, "col", None))
    return jax.shard_map(
        per_device, mesh=mesh, in_specs=in_specs, out_specs=out_specs, check_vma=False
    )
```

```python
import math

import jax
import jax.numpy as jnp
from jax import lax
from jax.experimental import pallas as pl
from jax.experimental.pallas import tpu as pltpu
from jax.sharding import PartitionSpec as P

D0 = 768
TILE = 256
PANELS = 2
SPAN = PANELS * TILE
BLOCK = 128
PIVOTS = 8
BIAS = 0.1
RIDGE = 0.1
TINY = 1e-30
EXACT = lax.Precision.HIGHEST
F32 = jnp.float32
BF16 = jnp.bfloat16

ARC = (
    0.30011410855430565,
    0.014911524637152361,
    0.0027575196411184027,
    4.221988638112521e-06,
    0.0005224396428474578,
)


def matmul(left, right, left_dim, right_dim, precision=None):
    return lax.dot_general(
        left, right, (((left_dim,), (right_dim,)), ((), ())), precision=precision,
        preferred_element_type=F32,
    )


def split(value):
    high = value.astype(BF16)
    return high, (value - high.astype(F32)).astype(BF16)


def arc_term(gap):
    series = ARC[4] * gap + ARC[3]
    for coefficient in ARC[2::-1]:
        series = series * gap + coefficient
    return gap * gap * lax.rsqrt(gap) * series


def scales(squares):
    d0 = squares * (1.0 / D0)
    d1 = d0 + BIAS
    d2 = d1 + BIAS
    inverse1 = lax.rsqrt(d1)
    inverse2 = lax.rsqrt(d2)
    root_bias = math.sqrt(BIAS)
    return (
        lax.rsqrt(squares),
        root_bias * inverse1,
        jnp.sqrt(d0) * inverse1,
        root_bias * inverse2,
        jnp.sqrt(d1) * inverse2,
        jnp.sqrt(d2),
    )


def layers(product, rows, columns):
    cosine = product * rows[0] * columns[0]
    gap = jnp.maximum(1.0 - jnp.abs(cosine), TINY)
    value = jnp.maximum(cosine, 0.0) + arc_term(gap)
    for layer in (1, 3):
        gap = 1.0 - rows[layer] * columns[layer]
        gap = jnp.maximum(gap - rows[layer + 1] * columns[layer + 1] * value, TINY)
        value = (1.0 - gap) + arc_term(gap)
    return rows[5] * columns[5] * value


def row_squares(block):
    wide = block.astype(F32)
    return jnp.sum(wide * wide, axis=1, keepdims=True)


def column_squares(block):
    return jnp.transpose(jnp.broadcast_to(row_squares(block), (block.shape[0], 128)))[0:1]


def unit(shape):
    return lax.broadcasted_iota(jnp.int32, shape, 0) == lax.broadcasted_iota(jnp.int32, shape, 1)


def store_scales(squares, out):
    for index, vector in enumerate(scales(squares)):
        out[index] = jnp.broadcast_to(vector, out.shape[1:])


def factor_block(block):
    count = BLOCK // 8
    nb = PIVOTS
    lane = lax.broadcasted_iota(jnp.int32, (8, BLOCK), 1)
    sub = lax.broadcasted_iota(jnp.int32, (8, BLOCK), 0)
    block = list(block)
    inverse = [jnp.where(lane == sub + 8 * g, 1.0, 0.0).astype(F32) for g in range(count)]

    def spread(value):
        return jnp.broadcast_to(value, (8, BLOCK))

    for k in range(0, BLOCK, nb):
        g0, s = k // 8, k % 8
        groups = range(g0 + 1 if s + nb == 8 else g0, count)
        columns = [[None] * count for _ in range(nb)]
        for j in range(nb):
            for g in range(g0, count):
                columns[j][g] = spread(block[g][:, k + j:k + j + 1])
        left = [spread(block[g0][s + j:s + j + 1, :]) for j in range(nb)]
        right = [spread(inverse[g0][s + j:s + j + 1, :]) for j in range(nb)]
        pivot = {
            (i, j): spread(columns[j][g0][s + i:s + i + 1, :])
            for j in range(nb) for i in range(j, nb)
        }
        reciprocal = []
        lower = {}
        for j in range(nb):
            reciprocal.append(1.0 / pivot[j, j])
            for i in range(j + 1, nb):
                lower[i, j] = pivot[i, j] * reciprocal[j]
            for m in range(j + 1, nb):
                for i in range(m, nb):
                    pivot[i, m] = pivot[i, m] - lower[i, j] * pivot[m, j]
        for i in range(nb):
            for j in range(i):
                left[i] = left[i] - lower[i, j] * left[j]
                right[i] = right[i] - lower[i, j] * right[j]
        for g in groups:
            for i in range(nb):
                for j in range(i):
                    columns[i][g] = columns[i][g] - lower[i, j] * columns[j][g]
        left = [left[i] * reciprocal[i] for i in range(nb)]
        scaled = [right[i] * reciprocal[i] for i in range(nb)]
        for g in groups:
            one, two = block[g], inverse[g]
            for i in range(nb):
                if k + nb < BLOCK:
                    one = one - columns[i][g] * left[i]
                two = two - columns[i][g] * scaled[i]
            if g == g0:
                below = sub >= s + nb
                one = jnp.where(below, one, block[g])
                two = jnp.where(below, two, inverse[g])
            block[g], inverse[g] = one, two
        done = inverse[g0]
        for i in range(nb):
            done = jnp.where(sub == s + i, right[i] * lax.rsqrt(pivot[i, i]), done)
        inverse[g0] = done
    return inverse


def invert_factor(matrix, inverse):
    count = SPAN // BLOCK
    inverse[...] = jnp.zeros((SPAN, SPAN), F32)
    for index in range(count):
        o = index * BLOCK
        e = o + BLOCK
        slabs = [matrix[o + 8 * g:o + 8 * g + 8, o:e] for g in range(BLOCK // 8)]
        own = jnp.concatenate(factor_block(slabs), axis=0)
        if index > 0:
            inverse[o:e, 0:o] = matmul(own, inverse[o:e, 0:o], 1, 0, EXACT)
        inverse[o:e, o:e] = own
        if index < count - 1:
            upper = matmul(own, matrix[o:e, e:SPAN], 1, 0, EXACT)
            matrix[e:SPAN, e:SPAN] -= matmul(upper, upper, 0, 0, EXACT)
            inverse[e:SPAN, 0:e] -= matmul(upper, inverse[o:e, 0:e], 0, 0, EXACT)


def choose_kernel(order, own, out):
    for k in range(PANELS):
        rows = own[order[k] // 16].astype(F32)
        for device in range(16):
            start = device % 4 * 8
            out[device, k] = rows[start:start + 8].astype(BF16)


def pick_kernel(order, came, out):
    for k in range(PANELS):
        rows = came[order[k] % 16, k]
        for device in range(16):
            out[device, k] = rows


def pivot_kernel(mine, other, panel, high_out, low_out, mean_out, mean_row_out, center_out, center_row_out,
                 scales_out, scales_row_out, matrix, inverse):
    core = lax.axis_index("col") % 2
    for source, side in ((mine, core), (other, 1 - core)):
        for k in range(PANELS):
            for x in range(4):
                for y in (0, 2):
                    rows = [source[(y + i) * 4 + x, k].astype(F32) for i in range(2)]
                    start = pl.multiple_of(k * TILE + 64 * x + 32 * side + 8 * y, 16)
                    panel[pl.ds(start, 16), :] = jnp.concatenate(rows, axis=0).astype(BF16)
    store_scales(row_squares(panel[...]), scales_out)
    for index, vector in enumerate(scales(column_squares(panel[...]))):
        scales_row_out[index] = vector
    for index in range(4):
        rows = slice(index * BLOCK, (index + 1) * BLOCK)
        product = matmul(panel[rows, :], panel[...], 1, 1)
        for lanes in range(4):
            columns = slice(lanes * BLOCK, (lanes + 1) * BLOCK)
            matrix[rows, columns] = BIAS + layers(
                product[:, columns],
                [scales_out[i, rows] for i in range(6)],
                [scales_row_out[i, :, columns] for i in range(6)],
            )
    mean_row = jnp.sum(matrix[...], axis=0, keepdims=True) * (1.0 / SPAN)
    mean_row_out[...] = mean_row
    mean = jnp.sum(matrix[...], axis=1, keepdims=True) * (1.0 / SPAN)
    mean_out[...] = jnp.broadcast_to(mean, mean_out.shape)
    matrix[...] += jnp.where(unit((SPAN, SPAN)), RIDGE, 0.0)
    invert_factor(matrix, inverse)
    high, low = split(inverse[...])
    high_out[...] = high
    low_out[...] = low
    center = jnp.sum(inverse[...] * mean_row, axis=1, keepdims=True)
    center_out[...] = jnp.broadcast_to(center, center_out.shape)
    center_row_out[...] = matmul(
        jnp.broadcast_to(mean_row, (8, SPAN)), inverse[...], 1, 1, EXACT
    )[0:1]


def eye_term(start, lanes, amount):
    row = lax.broadcasted_iota(jnp.int32, (64, 128), 0) + (start - lanes)
    return jnp.where(row == lax.broadcasted_iota(jnp.int32, (64, 128), 1), amount, 0.0)


def main_kernel(order, row_inputs, column_inputs, panel,
                high_in, low_in, mean, mean_row, center, center_row, panel_scales,
                panel_scales_row, factor_out, trailing_out,
                column_high, column_low, column_scales, column_shift,
                own, row_scales, row_high, row_low, row_factor,
                product0, product1, update0, update1, high0, high1, low0, low1):
    group = pl.program_id(0)
    row_position, column_position = lax.axis_index("row"), lax.axis_index("col")
    product, update = (product0, product1), (update0, update1)
    panel_high, panel_low = (high0, high1), (low0, low1)

    def column_block(p):
        return column_inputs[p % 2, :, p // 2].reshape(TILE, D0)

    def ridge_of(tile, index):
        return jnp.where(order[index] == tile, RIDGE, 0.0).astype(F32)

    def column_first(p, slot):
        block = column_block(p)
        product[slot][...] = matmul(panel[...], block, 1, 1)
        for index, vector in enumerate(scales(column_squares(block))):
            column_scales[p, index] = vector

    def column_middle(p, slot):
        for start in range(0, SPAN, 64):
            index = start // TILE
            ridge = ridge_of(p * 8 + column_position, index)
            rows = slice(start, start + 64)
            for lanes in (0, 128):
                wide = slice(lanes, lanes + 128)
                value = (BIAS - mean[rows]) + layers(
                    product[slot][rows, wide],
                    [panel_scales[i, rows] for i in range(6)],
                    [column_scales[p, i, :, wide] for i in range(6)],
                )
                if start % TILE // 128 * 128 == lanes:
                    value = value + eye_term(start % TILE, lanes, ridge)
                high, low = split(value)
                panel_high[slot][rows, wide] = high
                panel_low[slot][rows, wide] = low

    def column_last(p, slot):
        shift = 0.0
        for index in range(PANELS):
            rows = slice(index * TILE, (index + 1) * TILE)
            depth = (index + 1) * TILE
            high, low = panel_high[slot][:depth, :], panel_low[slot][:depth, :]
            factor = matmul(high_in[rows, :depth], high, 1, 0) + (
                matmul(high_in[rows, :depth], low, 1, 0) + matmul(low_in[rows, :depth], high, 1, 0)
            )
            weight = center[rows]
            shift = shift + jnp.sum(
                factor * jnp.concatenate([weight, weight], axis=1), axis=0, keepdims=True
            )
            high, low = split(factor)
            column_high[p, rows] = high
            column_low[p, rows] = low
        column_shift[p] = shift

    def row_first(q, slot):
        block = own[pl.ds(pl.multiple_of(q * TILE, TILE), TILE), :]
        for index in range(PANELS):
            rows = slice(index * TILE, (index + 1) * TILE)
            product[slot][rows, :] = matmul(block, panel[rows, :], 1, 1)

    def row_middle(q, slot):
        for index in range(PANELS):
            ridge = ridge_of(q * 16 + row_position, index)
            for start in range(0, TILE, 64):
                rows = pl.ds(pl.multiple_of(q * TILE + start, 64), 64)
                here = slice(index * TILE + start, index * TILE + start + 64)
                for lanes in (0, 128):
                    wide = slice(index * TILE + lanes, index * TILE + lanes + 128)
                    value = (BIAS - mean_row[:, wide]) + layers(
                        product[slot][here, lanes:lanes + 128],
                        [row_scales[i, rows] for i in range(6)],
                        [panel_scales_row[i, :, wide] for i in range(6)],
                    )
                    if start // 128 * 128 == lanes:
                        value = value + eye_term(start, lanes, ridge)
                    high, low = split(value)
                    panel_high[slot][here, lanes:lanes + 128] = high
                    panel_low[slot][here, lanes:lanes + 128] = low

    def row_last(q, slot):
        rows = pl.ds(pl.multiple_of(q * TILE, TILE), TILE)
        shift = BIAS - jnp.sum(center_row[...] * center_row[...], axis=1, keepdims=True)
        for index in range(PANELS):
            wide = slice(index * TILE, (index + 1) * TILE)
            factor = 0.0
            for part in range(index + 1):
                depth = slice(part * TILE, (part + 1) * TILE)
                high, low = panel_high[slot][depth, :], panel_low[slot][depth, :]
                factor = factor + (
                    matmul(high, high_in[wide, depth], 1, 1)
                    + (matmul(high, low_in[wide, depth], 1, 1) + matmul(low, high_in[wide, depth], 1, 1))
                )
            row_factor[rows, wide] = factor + center_row[:, wide]
            shift = shift - jnp.sum(factor * center_row[:, wide], axis=1, keepdims=True)
            high, low = split(factor)
            row_high[rows, wide] = high
            row_low[rows, wide] = low
        row_scales[6, rows] = jnp.broadcast_to(shift, (TILE, 128))

    def pipeline(count, first, middle, last):
        first(0, 0)

        def pair(step, _):
            for slot in range(2):
                at = step * 2 + slot
                last(jnp.maximum(at - 1, 0), 1 - slot)
                first(jnp.minimum(at + 1, count - 1), 1 - slot)
                middle(at, slot)
            return 0

        lax.fori_loop(0, count // 2, pair, 0)
        last(count - 1, 1)

    @pl.when(group == 0)
    def _():
        for q in range(4):
            own[q * TILE:(q + 1) * TILE, :] = row_inputs[:, q].reshape(TILE, D0)
        for start in range(0, 4 * TILE, 128):
            for index, vector in enumerate(scales(row_squares(own[start:start + 128, :]))):
                row_scales[index, start:start + 128] = jnp.broadcast_to(vector, (128, 128))
        pipeline(4, row_first, row_middle, row_last)
        pipeline(8, column_first, column_middle, column_last)

    for half in range(2):
        rows = pl.ds(pl.multiple_of(group * 2 * TILE + half * TILE, TILE), TILE)
        factor_out[half] = row_factor[rows, :]

    def tile_first(p, slot):
        rows = slice(slot * SPAN, (slot + 1) * SPAN)
        product[slot][...] = matmul(own[rows, :], column_block(p), 1, 1)
        update[slot][...] = matmul(row_high[rows, :], column_high[p], 1, 0) + (
            matmul(row_high[rows, :], column_low[p], 1, 0)
            + matmul(row_low[rows, :], column_high[p], 1, 0)
        )

    def tile_middle(p, slot):
        for start in range(0, SPAN, 64):
            here = slice(start, start + 64)
            rows = slice(slot * SPAN + start, slot * SPAN + start + 64)
            for half in range(2):
                wide = slice(half * 128, half * 128 + 128)
                value = layers(
                    product[slot][here, wide],
                    [row_scales[i, rows] for i in range(6)],
                    [column_scales[p, i, :, wide] for i in range(6)],
                )
                value = value + (row_scales[6, rows] - column_shift[p, :, wide])
                value = value - update[slot][here, wide]
                at = (slot * SPAN + start) * 8 + p % 4 * 2 + half
                trailing[pl.ds(at, 64, stride=8), :] = value

    trailing = trailing_out.reshape(4 * TILE * 8, 128)
    tile_first(group * 4, 0)

    def tile(step, _):
        p = group * 4 + step
        tile_first(p, 1)
        tile_middle(p, 0)
        tile_first(jnp.minimum(p + 1, 7), 0)
        tile_middle(p, 1)
        return 0

    lax.fori_loop(0, 4, tile, 0)

    @pl.when(row_position % 8 == column_position)
    def _():
        for part in range(2):
            q = group * 2 + part
            p = part * 2 + row_position // 8
            for start in range(0, TILE, 64):
                half = start // 128
                at = pl.ds(pl.multiple_of(q * TILE + start, 64), 64)
                trailing_out[at, p * 2 + half, :] += eye_term(start, half * 128, RIDGE)


def whole(shape):
    return pl.BlockSpec(shape, lambda *_: (0,) * len(shape))


def call_small(kernel, order, block, name):
    return pl.pallas_call(
        kernel,
        out_shape=jax.ShapeDtypeStruct((16, PANELS, 8, D0), BF16),
        in_specs=[pl.BlockSpec(memory_space=pltpu.SMEM), pl.BlockSpec(memory_space=pltpu.VMEM)],
        name=name,
    )(order, block)


def call_pivot(mine, other):
    shapes = [
        ((SPAN, D0), BF16),
        ((SPAN, SPAN), BF16), ((SPAN, SPAN), BF16), ((SPAN, 128), F32), ((1, SPAN), F32),
        ((SPAN, 128), F32), ((1, SPAN), F32), ((6, SPAN, 128), F32), ((6, 1, SPAN), F32),
    ]
    return pl.pallas_call(
        pivot_kernel,
        out_shape=[jax.ShapeDtypeStruct(s, d) for s, d in shapes],
        in_specs=[pl.BlockSpec(memory_space=pltpu.VMEM)] * 2,
        scratch_shapes=[pltpu.VMEM((SPAN, SPAN), F32), pltpu.VMEM((SPAN, SPAN), F32)],
        compiler_params=pltpu.CompilerParams(vmem_limit_bytes=60 * 2**20),
        cost_estimate=pl.CostEstimate(flops=3 * 10**10, bytes_accessed=4 * 10**6, transcendentals=0),
        name="pivot",
    )(mine, other)


def call_main(order, row_inputs, column_inputs, arrays):
    factor, trailing = pl.pallas_call(
        main_kernel,
        grid=(2,),
        out_shape=[
            jax.ShapeDtypeStruct((4, TILE, SPAN), F32),
            jax.ShapeDtypeStruct((4 * TILE, 16, 128), F32),
        ],
        in_specs=[pl.BlockSpec(memory_space=pltpu.SMEM)]
        + [pl.BlockSpec(memory_space=pltpu.VMEM)] * (2 + len(arrays)),
        out_specs=[
            pl.BlockSpec((2, TILE, SPAN), lambda g: (g, 0, 0)),
            pl.BlockSpec((4 * TILE, 8, 128), lambda g: (0, g, 0)),
        ],
        scratch_shapes=[
            pltpu.VMEM((8, SPAN, TILE), BF16),
            pltpu.VMEM((8, SPAN, TILE), BF16),
            pltpu.VMEM((8, 6, 1, TILE), F32),
            pltpu.VMEM((8, 1, TILE), F32),
            pltpu.VMEM((4 * TILE, D0), BF16),
            pltpu.VMEM((7, 4 * TILE, 128), F32),
            pltpu.VMEM((4 * TILE, SPAN), BF16),
            pltpu.VMEM((4 * TILE, SPAN), BF16),
            pltpu.VMEM((4 * TILE, SPAN), F32),
        ] + [pltpu.VMEM((SPAN, TILE), F32)] * 4 + [pltpu.VMEM((SPAN, TILE), BF16)] * 4,
        compiler_params=pltpu.CompilerParams(vmem_limit_bytes=60 * 2**20),
        name="main",
    )(order, row_inputs, column_inputs, *arrays)
    return factor, trailing


def exchange(block, axes, groups):
    return lax.all_to_all(block, axes, 0, 0, tiled=True, axis_index_groups=groups)


def per_device(inputs, panel_order):
    own = inputs[:, 0]
    row_count = lax.axis_size("row")
    column_count = lax.axis_size("col")
    turn = [
        (r * column_count + c, (column_count * (r // column_count) + c) * column_count + r % column_count)
        for r in range(row_count) for c in range(column_count)
    ]
    turned = lax.ppermute(own, ("row", "col"), turn)
    row_inputs = lax.all_gather(own, "col", axis=0)
    swap = [(c, c ^ 1) for c in range(column_count)]
    sent = call_small(choose_kernel, panel_order, own, "choose")
    came = exchange(sent, "row", None)
    came, turned = lax.optimization_barrier((came, turned))
    column_inputs = lax.all_gather(turned, "row", axis=0).reshape(2, 8, 4, 32, D0)
    piece = call_small(pick_kernel, panel_order, came, "pick")
    groups = [
        [(z * 4 + y) * column_count + 2 * x + core for y in range(4) for x in range(4)]
        for z in range(row_count // 4) for core in range(2)
    ]
    mine = exchange(piece, ("row", "col"), groups)
    other = lax.ppermute(mine, "col", swap)
    pivot = call_pivot(mine, other)
    factor, trailing = call_main(panel_order, row_inputs, column_inputs, pivot)
    return factor.reshape(4, 1, TILE, SPAN), trailing.reshape(4, 1, TILE, 8, 1, TILE)


def solution(mesh):
    in_specs = (P(None, "row", "col", None), P())
    out_specs = (P(None, "row", None, None), P(None, "row", None, None, "col", None))
    return jax.shard_map(
        per_device, mesh=mesh, in_specs=in_specs, out_specs=out_specs, check_vma=False
    )
```

```python
import math

import jax
import jax.numpy as jnp
from jax import lax
from jax.experimental import pallas as pl
from jax.experimental.pallas import tpu as pltpu
from jax.sharding import PartitionSpec as P

D0 = 768
TILE = 256
PANELS = 2
SPAN = PANELS * TILE
BLOCK = 128
PIVOTS = 8
BIAS = 0.1
RIDGE = 0.1
TINY = 1e-30
EXACT = lax.Precision.HIGHEST
F32 = jnp.float32
BF16 = jnp.bfloat16

ARC = (
    0.30011410855430565,
    0.014911524637152361,
    0.0027575196411184027,
    4.221988638112521e-06,
    0.0005224396428474578,
)


def matmul(left, right, left_dim, right_dim, precision=None):
    return lax.dot_general(
        left, right, (((left_dim,), (right_dim,)), ((), ())), precision=precision,
        preferred_element_type=F32,
    )


def split(value):
    high = value.astype(BF16)
    return high, (value - high.astype(F32)).astype(BF16)


def arc_term(gap):
    series = ARC[4] * gap + ARC[3]
    for coefficient in ARC[2::-1]:
        series = series * gap + coefficient
    return gap * gap * lax.rsqrt(gap) * series


def scales(squares):
    d0 = squares * (1.0 / D0)
    d1 = d0 + BIAS
    d2 = d1 + BIAS
    inverse1 = lax.rsqrt(d1)
    inverse2 = lax.rsqrt(d2)
    root_bias = math.sqrt(BIAS)
    return (
        lax.rsqrt(squares),
        root_bias * inverse1,
        jnp.sqrt(d0) * inverse1,
        root_bias * inverse2,
        jnp.sqrt(d1) * inverse2,
        jnp.sqrt(d2),
    )


def layers(product, rows, columns):
    cosine = product * rows[0] * columns[0]
    gap = jnp.maximum(1.0 - jnp.abs(cosine), TINY)
    value = jnp.maximum(cosine, 0.0) + arc_term(gap)
    for layer in (1, 3):
        gap = 1.0 - rows[layer] * columns[layer]
        gap = jnp.maximum(gap - rows[layer + 1] * columns[layer + 1] * value, TINY)
        value = (1.0 - gap) + arc_term(gap)
    return rows[5] * columns[5] * value


def row_squares(block):
    wide = block.astype(F32)
    return jnp.sum(wide * wide, axis=1, keepdims=True)


def column_squares(block):
    return jnp.transpose(jnp.broadcast_to(row_squares(block), (block.shape[0], 128)))[0:1]


def unit(shape):
    return lax.broadcasted_iota(jnp.int32, shape, 0) == lax.broadcasted_iota(jnp.int32, shape, 1)


def store_scales(squares, out):
    for index, vector in enumerate(scales(squares)):
        out[index] = jnp.broadcast_to(vector, out.shape[1:])


def factor_block(block):
    count = BLOCK // 8
    nb = PIVOTS
    lane = lax.broadcasted_iota(jnp.int32, (8, BLOCK), 1)
    sub = lax.broadcasted_iota(jnp.int32, (8, BLOCK), 0)
    block = list(block)
    inverse = [jnp.where(lane == sub + 8 * g, 1.0, 0.0).astype(F32) for g in range(count)]

    def spread(value):
        return jnp.broadcast_to(value, (8, BLOCK))

    for k in range(0, BLOCK, nb):
        g0, s = k // 8, k % 8
        groups = range(g0 + 1 if s + nb == 8 else g0, count)
        columns = [[None] * count for _ in range(nb)]
        for j in range(nb):
            for g in range(g0, count):
                columns[j][g] = spread(block[g][:, k + j:k + j + 1])
        left = [spread(block[g0][s + j:s + j + 1, :]) for j in range(nb)]
        right = [spread(inverse[g0][s + j:s + j + 1, :]) for j in range(nb)]
        pivot = {
            (i, j): spread(columns[j][g0][s + i:s + i + 1, :])
            for j in range(nb) for i in range(j, nb)
        }
        reciprocal = []
        lower = {}
        for j in range(nb):
            reciprocal.append(1.0 / pivot[j, j])
            for i in range(j + 1, nb):
                lower[i, j] = pivot[i, j] * reciprocal[j]
            for m in range(j + 1, nb):
                for i in range(m, nb):
                    pivot[i, m] = pivot[i, m] - lower[i, j] * pivot[m, j]
        for i in range(nb):
            for j in range(i):
                left[i] = left[i] - lower[i, j] * left[j]
                right[i] = right[i] - lower[i, j] * right[j]
        for g in groups:
            for i in range(nb):
                for j in range(i):
                    columns[i][g] = columns[i][g] - lower[i, j] * columns[j][g]
        left = [left[i] * reciprocal[i] for i in range(nb)]
        scaled = [right[i] * reciprocal[i] for i in range(nb)]
        for g in groups:
            one, two = block[g], inverse[g]
            for i in range(nb):
                if k + nb < BLOCK:
                    one = one - columns[i][g] * left[i]
                two = two - columns[i][g] * scaled[i]
            if g == g0:
                below = sub >= s + nb
                one = jnp.where(below, one, block[g])
                two = jnp.where(below, two, inverse[g])
            block[g], inverse[g] = one, two
        done = inverse[g0]
        for i in range(nb):
            done = jnp.where(sub == s + i, right[i] * lax.rsqrt(pivot[i, i]), done)
        inverse[g0] = done
    return inverse


def invert_factor(matrix, inverse):
    count = SPAN // BLOCK
    inverse[...] = jnp.zeros((SPAN, SPAN), F32)
    for index in range(count):
        o = index * BLOCK
        e = o + BLOCK
        slabs = [matrix[o + 8 * g:o + 8 * g + 8, o:e] for g in range(BLOCK // 8)]
        own = jnp.concatenate(factor_block(slabs), axis=0)
        if index > 0:
            inverse[o:e, 0:o] = matmul(own, inverse[o:e, 0:o], 1, 0, EXACT)
        inverse[o:e, o:e] = own
        if index < count - 1:
            upper = matmul(own, matrix[o:e, e:SPAN], 1, 0, EXACT)
            matrix[e:SPAN, e:SPAN] -= matmul(upper, upper, 0, 0, EXACT)
            inverse[e:SPAN, 0:e] -= matmul(upper, inverse[o:e, 0:e], 0, 0, EXACT)


def choose_kernel(order, own, out):
    for k in range(PANELS):
        rows = own[order[k] // 16].astype(F32)
        for device in range(16):
            start = device % 4 * 8
            out[device, k] = rows[start:start + 8].astype(BF16)


def pick_kernel(order, came, out):
    for k in range(PANELS):
        rows = came[order[k] % 16, k]
        for device in range(16):
            out[device, k] = rows


def pivot_kernel(mine, other, panel, high_out, low_out, mean_out, mean_row_out, center_out, center_row_out,
                 scales_out, scales_row_out, matrix, inverse):
    core = lax.axis_index("col") % 2
    for source, side in ((mine, core), (other, 1 - core)):
        for k in range(PANELS):
            for x in range(4):
                for y in (0, 2):
                    rows = [source[(y + i) * 4 + x, k].astype(F32) for i in range(2)]
                    start = pl.multiple_of(k * TILE + 64 * x + 32 * side + 8 * y, 16)
                    panel[pl.ds(start, 16), :] = jnp.concatenate(rows, axis=0).astype(BF16)
    store_scales(row_squares(panel[...]), scales_out)
    for index, vector in enumerate(scales(column_squares(panel[...]))):
        scales_row_out[index] = vector
    for index in range(4):
        rows = slice(index * BLOCK, (index + 1) * BLOCK)
        product = matmul(panel[rows, :], panel[...], 1, 1)
        for lanes in range(4):
            columns = slice(lanes * BLOCK, (lanes + 1) * BLOCK)
            matrix[rows, columns] = BIAS + layers(
                product[:, columns],
                [scales_out[i, rows] for i in range(6)],
                [scales_row_out[i, :, columns] for i in range(6)],
            )
    mean_row = jnp.sum(matrix[...], axis=0, keepdims=True) * (1.0 / SPAN)
    mean_row_out[...] = mean_row
    mean = jnp.sum(matrix[...], axis=1, keepdims=True) * (1.0 / SPAN)
    mean_out[...] = jnp.broadcast_to(mean, mean_out.shape)
    matrix[...] += jnp.where(unit((SPAN, SPAN)), RIDGE, 0.0)
    invert_factor(matrix, inverse)
    high, low = split(inverse[...])
    high_out[...] = high
    low_out[...] = low
    center = jnp.sum(inverse[...] * mean_row, axis=1, keepdims=True)
    center_out[...] = jnp.broadcast_to(center, center_out.shape)
    center_row_out[...] = matmul(
        jnp.broadcast_to(mean_row, (8, SPAN)), inverse[...], 1, 1, EXACT
    )[0:1]


def eye_term(start, lanes, amount):
    row = lax.broadcasted_iota(jnp.int32, (64, 128), 0) + (start - lanes)
    return jnp.where(row == lax.broadcasted_iota(jnp.int32, (64, 128), 1), amount, 0.0)


def main_kernel(order, row_inputs, column_inputs, panel,
                high_in, low_in, mean, mean_row, center, center_row, panel_scales,
                panel_scales_row, factor_out, trailing_out,
                column_high, column_low, column_scales, column_shift,
                own, row_scales, row_high, row_low, row_factor,
                product0, product1, update0, update1, high0, high1, low0, low1):
    group = pl.program_id(0)
    row_position, column_position = lax.axis_index("row"), lax.axis_index("col")
    product, update = (product0, product1), (update0, update1)
    panel_high, panel_low = (high0, high1), (low0, low1)

    def column_block(p):
        return column_inputs[p % 2, :, p // 2].reshape(TILE, D0)

    def ridge_of(tile, index):
        return jnp.where(order[index] == tile, RIDGE, 0.0).astype(F32)

    def column_first(p, slot):
        block = column_block(p)
        product[slot][...] = matmul(panel[...], block, 1, 1)
        for index, vector in enumerate(scales(column_squares(block))):
            column_scales[p, index] = vector

    def column_middle(p, slot):
        for start in range(0, SPAN, 64):
            index = start // TILE
            ridge = ridge_of(p * 8 + column_position, index)
            rows = slice(start, start + 64)
            for lanes in (0, 128):
                wide = slice(lanes, lanes + 128)
                value = (BIAS - mean[rows]) + layers(
                    product[slot][rows, wide],
                    [panel_scales[i, rows] for i in range(6)],
                    [column_scales[p, i, :, wide] for i in range(6)],
                )
                if start % TILE // 128 * 128 == lanes:
                    value = value + eye_term(start % TILE, lanes, ridge)
                high, low = split(value)
                panel_high[slot][rows, wide] = high
                panel_low[slot][rows, wide] = low

    def column_last(p, slot):
        shift = 0.0
        for index in range(PANELS):
            rows = slice(index * TILE, (index + 1) * TILE)
            depth = (index + 1) * TILE
            high, low = panel_high[slot][:depth, :], panel_low[slot][:depth, :]
            factor = matmul(high_in[rows, :depth], high, 1, 0) + (
                matmul(high_in[rows, :depth], low, 1, 0) + matmul(low_in[rows, :depth], high, 1, 0)
            )
            weight = center[rows]
            shift = shift + jnp.sum(
                factor * jnp.concatenate([weight, weight], axis=1), axis=0, keepdims=True
            )
            high, low = split(factor)
            column_high[p, rows] = high
            column_low[p, rows] = low
        column_shift[p] = shift

    def row_first(q, slot):
        block = own[pl.ds(pl.multiple_of(q * TILE, TILE), TILE), :]
        for index in range(PANELS):
            rows = slice(index * TILE, (index + 1) * TILE)
            product[slot][rows, :] = matmul(block, panel[rows, :], 1, 1)

    def row_middle(q, slot):
        for index in range(PANELS):
            ridge = ridge_of(q * 16 + row_position, index)
            for start in range(0, TILE, 64):
                rows = pl.ds(pl.multiple_of(q * TILE + start, 64), 64)
                here = slice(index * TILE + start, index * TILE + start + 64)
                for lanes in (0, 128):
                    wide = slice(index * TILE + lanes, index * TILE + lanes + 128)
                    value = (BIAS - mean_row[:, wide]) + layers(
                        product[slot][here, lanes:lanes + 128],
                        [row_scales[i, rows] for i in range(6)],
                        [panel_scales_row[i, :, wide] for i in range(6)],
                    )
                    if start // 128 * 128 == lanes:
                        value = value + eye_term(start, lanes, ridge)
                    high, low = split(value)
                    panel_high[slot][here, lanes:lanes + 128] = high
                    panel_low[slot][here, lanes:lanes + 128] = low

    def row_last(q, slot):
        rows = pl.ds(pl.multiple_of(q * TILE, TILE), TILE)
        shift = BIAS - jnp.sum(center_row[...] * center_row[...], axis=1, keepdims=True)
        for index in range(PANELS):
            wide = slice(index * TILE, (index + 1) * TILE)
            factor = 0.0
            for part in range(index + 1):
                depth = slice(part * TILE, (part + 1) * TILE)
                high, low = panel_high[slot][depth, :], panel_low[slot][depth, :]
                factor = factor + (
                    matmul(high, high_in[wide, depth], 1, 1)
                    + (matmul(high, low_in[wide, depth], 1, 1) + matmul(low, high_in[wide, depth], 1, 1))
                )
            row_factor[rows, wide] = factor + center_row[:, wide]
            shift = shift - jnp.sum(factor * center_row[:, wide], axis=1, keepdims=True)
            high, low = split(factor)
            row_high[rows, wide] = high
            row_low[rows, wide] = low
        row_scales[6, rows] = jnp.broadcast_to(shift, (TILE, 128))

    def pipeline(count, first, middle, last):
        first(0, 0)

        def pair(step, _):
            for slot in range(2):
                at = step * 2 + slot
                last(jnp.maximum(at - 1, 0), 1 - slot)
                first(jnp.minimum(at + 1, count - 1), 1 - slot)
                middle(at, slot)
            return 0

        lax.fori_loop(0, count // 2, pair, 0)
        last(count - 1, 1)

    @pl.when(group == 0)
    def _():
        for q in range(4):
            own[q * TILE:(q + 1) * TILE, :] = row_inputs[:, q].reshape(TILE, D0)
        for start in range(0, 4 * TILE, 128):
            for index, vector in enumerate(scales(row_squares(own[start:start + 128, :]))):
                row_scales[index, start:start + 128] = jnp.broadcast_to(vector, (128, 128))
        pipeline(4, row_first, row_middle, row_last)
        pipeline(8, column_first, column_middle, column_last)

    for half in range(2):
        rows = pl.ds(pl.multiple_of(group * 2 * TILE + half * TILE, TILE), TILE)
        factor_out[half] = row_factor[rows, :]

    def tile_first(p, slot):
        rows = slice(slot * SPAN, (slot + 1) * SPAN)
        product[slot][...] = matmul(own[rows, :], column_block(p), 1, 1)
        update[slot][...] = matmul(row_high[rows, :], column_high[p], 1, 0) + (
            matmul(row_high[rows, :], column_low[p], 1, 0)
            + matmul(row_low[rows, :], column_high[p], 1, 0)
        )

    def tile_middle(p, slot):
        for start in range(0, SPAN, 64):
            here = slice(start, start + 64)
            rows = slice(slot * SPAN + start, slot * SPAN + start + 64)
            for half in range(2):
                wide = slice(half * 128, half * 128 + 128)
                value = layers(
                    product[slot][here, wide],
                    [row_scales[i, rows] for i in range(6)],
                    [column_scales[p, i, :, wide] for i in range(6)],
                )
                value = value + (row_scales[6, rows] - column_shift[p, :, wide])
                value = value - update[slot][here, wide]
                at = (slot * SPAN + start) * 8 + p % 4 * 2 + half
                trailing[pl.ds(at, 64, stride=8), :] = value

    trailing = trailing_out.reshape(4 * TILE * 8, 128)
    tile_first(group * 4, 0)

    def tile(step, _):
        p = group * 4 + step
        tile_first(p, 1)
        tile_middle(p, 0)
        tile_first(jnp.minimum(p + 1, 7), 0)
        tile_middle(p, 1)
        return 0

    lax.fori_loop(0, 4, tile, 0)

    @pl.when(row_position % 8 == column_position)
    def _():
        for part in range(2):
            q = group * 2 + part
            p = part * 2 + row_position // 8
            for start in range(0, TILE, 64):
                half = start // 128
                at = pl.ds(pl.multiple_of(q * TILE + start, 64), 64)
                trailing_out[at, p * 2 + half, :] += eye_term(start, half * 128, RIDGE)


def whole(shape):
    return pl.BlockSpec(shape, lambda *_: (0,) * len(shape))


def call_small(kernel, order, block, name):
    return pl.pallas_call(
        kernel,
        out_shape=jax.ShapeDtypeStruct((16, PANELS, 8, D0), BF16),
        in_specs=[pl.BlockSpec(memory_space=pltpu.SMEM), pl.BlockSpec(memory_space=pltpu.VMEM)],
        name=name,
    )(order, block)


def call_pivot(mine, other):
    shapes = [
        ((SPAN, D0), BF16),
        ((SPAN, SPAN), BF16), ((SPAN, SPAN), BF16), ((SPAN, 128), F32), ((1, SPAN), F32),
        ((SPAN, 128), F32), ((1, SPAN), F32), ((6, SPAN, 128), F32), ((6, 1, SPAN), F32),
    ]
    return pl.pallas_call(
        pivot_kernel,
        out_shape=[jax.ShapeDtypeStruct(s, d) for s, d in shapes],
        in_specs=[pl.BlockSpec(memory_space=pltpu.VMEM)] * 2,
        scratch_shapes=[pltpu.VMEM((SPAN, SPAN), F32), pltpu.VMEM((SPAN, SPAN), F32)],
        compiler_params=pltpu.CompilerParams(vmem_limit_bytes=60 * 2**20),
        cost_estimate=pl.CostEstimate(flops=3 * 10**10, bytes_accessed=4 * 10**6, transcendentals=0),
        name="pivot",
    )(mine, other)


def call_main(order, row_inputs, column_inputs, arrays):
    factor, trailing = pl.pallas_call(
        main_kernel,
        grid=(2,),
        out_shape=[
            jax.ShapeDtypeStruct((4, TILE, SPAN), F32),
            jax.ShapeDtypeStruct((4 * TILE, 16, 128), F32),
        ],
        in_specs=[pl.BlockSpec(memory_space=pltpu.SMEM)]
        + [pl.BlockSpec(memory_space=pltpu.VMEM)] * (2 + len(arrays)),
        out_specs=[
            pl.BlockSpec((2, TILE, SPAN), lambda g: (g, 0, 0)),
            pl.BlockSpec((4 * TILE, 8, 128), lambda g: (0, g, 0)),
        ],
        scratch_shapes=[
            pltpu.VMEM((8, SPAN, TILE), BF16),
            pltpu.VMEM((8, SPAN, TILE), BF16),
            pltpu.VMEM((8, 6, 1, TILE), F32),
            pltpu.VMEM((8, 1, TILE), F32),
            pltpu.VMEM((4 * TILE, D0), BF16),
            pltpu.VMEM((7, 4 * TILE, 128), F32),
            pltpu.VMEM((4 * TILE, SPAN), BF16),
            pltpu.VMEM((4 * TILE, SPAN), BF16),
            pltpu.VMEM((4 * TILE, SPAN), F32),
        ] + [pltpu.VMEM((SPAN, TILE), F32)] * 4 + [pltpu.VMEM((SPAN, TILE), BF16)] * 4,
        compiler_params=pltpu.CompilerParams(vmem_limit_bytes=46 * 2**20),
        name="main",
    )(order, row_inputs, column_inputs, *arrays)
    return factor, trailing


def exchange(block, axes, groups):
    return lax.all_to_all(block, axes, 0, 0, tiled=True, axis_index_groups=groups)


def per_device(inputs, panel_order):
    own = inputs[:, 0]
    row_count = lax.axis_size("row")
    column_count = lax.axis_size("col")
    turn = [
        (r * column_count + c, (column_count * (r // column_count) + c) * column_count + r % column_count)
        for r in range(row_count) for c in range(column_count)
    ]
    turned = lax.ppermute(own, ("row", "col"), turn)
    row_inputs = lax.all_gather(own, "col", axis=0)
    swap = [(c, c ^ 1) for c in range(column_count)]
    sent = call_small(choose_kernel, panel_order, own, "choose")
    came = exchange(sent, "row", None)
    came, turned = lax.optimization_barrier((came, turned))
    column_inputs = lax.all_gather(turned, "row", axis=0).reshape(2, 8, 4, 32, D0)
    piece = call_small(pick_kernel, panel_order, came, "pick")
    groups = [
        [(z * 4 + y) * column_count + 2 * x + core for y in range(4) for x in range(4)]
        for z in range(row_count // 4) for core in range(2)
    ]
    mine = exchange(piece, ("row", "col"), groups)
    other = lax.ppermute(mine, "col", swap)
    pivot = call_pivot(mine, other)
    factor, trailing = call_main(panel_order, row_inputs, column_inputs, pivot)
    return factor.reshape(4, 1, TILE, SPAN), trailing.reshape(4, 1, TILE, 8, 1, TILE)


def solution(mesh):
    in_specs = (P(None, "row", "col", None), P())
    out_specs = (P(None, "row", None, None), P(None, "row", None, None, "col", None))
    return jax.shard_map(
        per_device, mesh=mesh, in_specs=in_specs, out_specs=out_specs, check_vma=False
    )
```
